512 devices in a mesh: fsdp: 32 (over y, x, core), expert: 16 (over z).
Axes of the slice: x: 4, y: 4, z: 16, core: 2. Of those that a mesh axis runs over, the one named last changes fastest.
Arguments:
- tokens: bfloat16 [65536, 2048], P(('fsdp', 'expert')), may hold values from -6 to 6
- cotangent: bfloat16 [65536, 2048], P(('fsdp', 'expert')), may hold values from -6 to 6
- routes: int32 [65536, 8], P(('fsdp', 'expert')), may hold values from 0 to 127, all different within a row
- route_weights: float32 [65536, 8], P(('fsdp', 'expert')), may hold values from 0.05 to 0.8
- gate_up_weight: bfloat16 [16, 2048, 1536], P('expert', 'fsdp'), may hold values from -0.125 to 0.125
- down_weight: bfloat16 [16, 2048, 768], P('expert', 'fsdp'), may hold values from -0.21875 to 0.21875
Outputs:
- mixed: bfloat16 [65536, 2048], P(('fsdp', 'expert'))
- grad_tokens: bfloat16 [65536, 2048], P(('fsdp', 'expert'))
- grad_gates: float32 [65536, 8], P(('fsdp', 'expert'))
The draws below stay inside these ranges and needn't reach their ends.
Inputs may be any that keep to these rules, and one draw needn't show every extreme that they name: `routes`: each row names 8 different experts.
All inputs are finite; a program needn't handle non-finite values.
Results may differ from the reference program's by a relative error of at most 0.0062.
Values may be sent and summed in bfloat16 or wider, within the bound.
A program may use at most 64 MiB of HBM per device.

```python
import math
import jax
import jax.numpy as jnp
from jax import lax

D = 2048
FF = 768
EXPERTS = 128
TOP = 8
TOK_DEV = 128
CAP = 12
EXP_GROUP = 16
TOKENS = 65536


def level_of(key, shape, split, smallest, largest):
    gain = 1.0
    for dim, blocks in split:
        steps = jax.random.uniform(jax.random.fold_in(jax.random.fold_in(key, 6), dim), (blocks,), jnp.float32, smallest / len(split), largest / len(split))
        gain = gain * jnp.repeat(jnp.exp(steps), shape[dim] // blocks).reshape((-1,) + (1,) * (len(shape) - 1 - dim))
    return gain


def picks_of(stream_key, rows, count, top, lift):
    sequence = jax.random.permutation(jax.random.fold_in(stream_key, 1), count)
    boost = sequence
    for power in range(3):
        boost = boost * boost // count
    boost = boost * lift // count
    tickets = jax.random.randint(jax.random.fold_in(stream_key, 2), (rows, count), 0, 4096) + boost
    sure = jax.random.permutation(jax.random.fold_in(stream_key, 3), rows)[jnp.arange(count) % rows]
    tickets = jnp.where(jnp.arange(rows)[:, None] == sure[None, :], 1 << 14, tickets)
    merit = tickets * count + jnp.arange(count)
    return lax.top_k(merit.astype(jnp.int32), top)[1].astype(jnp.int32)


def noise(rng, dims, width, bound, shards=(), held_as=jnp.bfloat16):
    factor_of = level_of(rng, dims, shards, -0.22, 0.18) if shards else 1.0
    result = jax.random.normal(rng, dims, jnp.float32) * width * factor_of
    return jnp.minimum(jnp.maximum(result, -bound), bound).astype(held_as)


def setup_inputs(seed: int = 0) -> dict:
    seeds = jax.random.split(jax.random.key(seed), 7)
    tokens = noise(seeds[0], (TOKENS, D), 1.0, 6.0, ((0, 512),))
    cotangent = noise(seeds[1], (TOKENS, D), 1.0, 6.0, ((0, 512),))
    routes = picks_of(seeds[2], TOKENS, EXPERTS, TOP, 512)
    route_weights = jnp.clip(jnp.exp(math.log(0.8) - 2.7725887 * jax.random.uniform(seeds[3], (TOKENS, TOP), jnp.float32) ** level_of(seeds[3], (TOKENS, TOP), ((0, 512),), -0.2, 0.2)), 0.05, 0.8)
    gate_up_weight = noise(seeds[4], (EXP_GROUP, D, 2 * FF), D ** -0.5, 0.125, ((0, 16), (1, 32)))
    down_weight = noise(seeds[5], (EXP_GROUP, D, FF), FF ** -0.5, 0.21875, ((0, 16), (1, 32)))
    return {"tokens": tokens, "cotangent": cotangent, "routes": routes, "route_weights": route_weights, "gate_up_weight": gate_up_weight, "down_weight": down_weight}


def slot_places(routes):
    blocks = routes.reshape(-1, TOK_DEV, TOP)
    block_count = blocks.shape[0]
    experts = jnp.arange(EXP_GROUP, dtype=jnp.int32)
    matches = (blocks[:, :, :, None] == experts).astype(jnp.int32)
    counts = jnp.sum(matches, axis=2, dtype=jnp.int32)
    earlier = jnp.cumsum(counts, axis=1, dtype=jnp.int32) - counts
    slot_ids = jnp.sum(matches * earlier[:, :, None, :], axis=3, dtype=jnp.int32)
    is_kept = (blocks < EXP_GROUP) & (slot_ids < CAP)
    block_ids = jnp.arange(block_count, dtype=jnp.int32)[:, None, None]
    places = (blocks * block_count + block_ids) * CAP + slot_ids
    places = jnp.where(is_kept, places, EXP_GROUP * block_count * CAP)
    return places.reshape(-1).astype(jnp.int32), block_count


def reference(tokens, cotangent, routes, route_weights, gate_up_weight, down_weight):
    places, block_count = slot_places(routes)
    per_expert = block_count * CAP
    total_slots = EXP_GROUP * per_expert
    token_ids = jnp.repeat(jnp.arange(TOKENS, dtype=jnp.int32), TOP)
    pair_ids = jnp.arange(TOKENS * TOP, dtype=jnp.int32)
    owners = jnp.full((total_slots + 1,), TOKENS, jnp.int32).at[places].set(token_ids)[:total_slots]
    pairs = jnp.full((total_slots + 1,), TOKENS * TOP, jnp.int32).at[places].set(pair_ids)[:total_slots]
    slot_weights = jnp.zeros((total_slots + 1,), jnp.float32).at[places].set(route_weights.reshape(-1))[:total_slots]
    blank_row = jnp.zeros((1, D), jnp.bfloat16)
    padded_tokens = jnp.concatenate([tokens, blank_row], 0)
    padded_cot = jnp.concatenate([cotangent, blank_row], 0)

    def expert_step(totals, inputs):
        mixed_sum, grad_sum, gate_grads = totals
        owner_rows, pair_rows, weight_rows, gate_up_mat, down_mat = inputs
        expert_rows = padded_tokens[owner_rows]
        cot_rows = padded_cot[owner_rows].astype(jnp.float32)
        routed_grads = (weight_rows[:, None] * cot_rows).astype(jnp.bfloat16)
        gate_up = jnp.dot(expert_rows, gate_up_mat, preferred_element_type=jnp.float32)
        gate_part = gate_up[:, :FF]
        up_part = gate_up[:, FF:]
        hidden = (jax.nn.silu(gate_part) * up_part).astype(jnp.bfloat16)
        expert_out = jnp.dot(hidden, down_mat.T, preferred_element_type=jnp.float32).astype(jnp.bfloat16)
        out_float = expert_out.astype(jnp.float32)
        mixed_sum = mixed_sum.at[owner_rows].add(weight_rows[:, None] * out_float, mode="drop")
        gate_grads = gate_grads.at[pair_rows].add(jnp.sum(out_float * cot_rows, axis=1), mode="drop")
        grad_hidden = jnp.dot(routed_grads, down_mat, preferred_element_type=jnp.float32)
        sigmoid_gate = jax.nn.sigmoid(gate_part)
        grad_gate = grad_hidden * up_part * sigmoid_gate * (1.0 + gate_part * (1.0 - sigmoid_gate))
        grad_up = grad_hidden * gate_part * sigmoid_gate
        grad_gate_up = jnp.concatenate([grad_gate, grad_up], 1).astype(jnp.bfloat16)
        expert_grad = jnp.dot(grad_gate_up, gate_up_mat.T, preferred_element_type=jnp.float32).astype(jnp.bfloat16)
        grad_sum = grad_sum.at[owner_rows].add(expert_grad.astype(jnp.float32), mode="drop")
        return (mixed_sum, grad_sum, gate_grads), None

    start = (jnp.zeros((TOKENS, D), jnp.float32), jnp.zeros((TOKENS, D), jnp.float32), jnp.zeros((TOKENS * TOP,), jnp.float32))
    inputs = (owners.reshape(EXP_GROUP, per_expert), pairs.reshape(EXP_GROUP, per_expert), slot_weights.reshape(EXP_GROUP, per_expert), gate_up_weight, down_weight)
    finals, unused = lax.scan(expert_step, start, inputs)
    mixed_sum, grad_sum, gate_grads = finals
    return mixed_sum.astype(jnp.bfloat16), grad_sum.astype(jnp.bfloat16), gate_grads.reshape(TOKENS, TOP)
```

```python
import functools

import jax
import jax.numpy as jnp
from jax import lax
from jax.experimental import pallas as pl
from jax.experimental.pallas import tpu as pltpu
from jax.sharding import PartitionSpec as P

MESH = pl.DeviceIdType.MESH
SLOTS = 16
GU_PIECE = 16
DN_PIECE = 32
NT = (((1,), (1,)), ((), ()))


def dot(a, b):
    return jnp.dot(a, b, preferred_element_type=jnp.float32)


def dot_nt(a, b):
    return lax.dot_general(a, b, NT, preferred_element_type=jnp.float32)


def rows_of(start, size):
    return pl.ds(pl.multiple_of(start, size), size)


def kernel(
    n,
    capacity,
    tokens,
    cotangent,
    routes,
    route_weights,
    gu_shard,
    dn_shard,
    mixed,
    grad_tokens,
    grad_gates,
    gu,
    dn,
    send_t,
    send_g,
    in_t,
    in_g,
    gate,
    up,
    hidden,
    ggu,
    out_s,
    eg_s,
    back_o,
    back_g,
    gu_recv,
    dn_recv,
    sib_gu,
    sib_dn,
    ring_send,
    sib_send,
    shard_send,
    row_recv,
    row_send,
    back_recv,
    back_send,
):
    tok_rows, width = tokens.shape
    top = routes.shape[1]
    shard = gu_shard.shape[1]
    ff = dn_shard.shape[2]
    slots = n * SLOTS
    sources = n
    half = width // 2
    gu_pieces = shard // GU_PIECE
    dn_pieces = shard // DN_PIECE
    me = lax.axis_index("fsdp")
    z = lax.axis_index("expert")
    q = me // 2
    core = lax.rem(me, 2)
    sibling = me + 1 - 2 * core
    after = lax.rem(z + 1 + core * (n - 2), n)
    before = lax.rem(z + n - 1 - core * (n - 2), n)
    passes_on = after != q

    barrier = pltpu.get_barrier_semaphore()

    def greet(k, carry):
        pl.semaphore_signal(
            barrier, inc=1, device_id=(lax.rem(me + k, 2 * n), z), device_id_type=MESH
        )
        return carry

    pl.semaphore_signal(barrier, inc=1, device_id=(me, after), device_id_type=MESH)
    pl.semaphore_signal(barrier, inc=1, device_id=(me, before), device_id_type=MESH)
    lax.fori_loop(1, 2 * n, greet, 0)

    lane = lax.broadcasted_iota(jnp.int32, (tok_rows, slots), 1)
    expert_of = lane // SLOTS
    slot_of = lane - expert_of * SLOTS
    weight_of = jnp.zeros((tok_rows, slots), jnp.float32)
    named = jnp.zeros((tok_rows, slots), jnp.float32)
    for k in range(top):
        hit = routes[:, k : k + 1] == expert_of
        named = jnp.where(hit, 1.0, named)
        weight_of = jnp.where(hit, route_weights[:, k : k + 1], weight_of)
    row_id = lax.broadcasted_iota(jnp.int32, (tok_rows, tok_rows), 0)
    col_id = lax.broadcasted_iota(jnp.int32, (tok_rows, tok_rows), 1)
    below = jnp.where(col_id < row_id, 1.0, 0.0).astype(jnp.bfloat16)
    earlier = dot(below, named.astype(jnp.bfloat16)).astype(jnp.int32)
    kept = (named > 0.5) & (earlier == slot_of) & (slot_of < capacity)
    chosen = jnp.where(kept, 1.0, 0.0)
    weight_of = jnp.where(kept, weight_of, 0.0)
    picks = jnp.transpose(chosen).astype(jnp.bfloat16)
    slot_weight = jnp.sum(jnp.transpose(weight_of), axis=1, keepdims=True)
    send_t[...] = dot(picks, tokens[...]).astype(jnp.bfloat16)
    send_g[...] = (slot_weight * dot(picks, cotangent[...])).astype(jnp.bfloat16)

    pl.semaphore_wait(barrier, 2 * n + 1)

    target = 2 * z + q // (n // 2)
    index = me - (q // (n // 2)) * sources

    def gu_piece(p):
        place = gu.at[rows_of(me * shard + p * GU_PIECE, GU_PIECE), :]
        return gu_shard.at[0, pl.ds(p * GU_PIECE, GU_PIECE), :], place, gu_recv.at[p * sources + index]

    def dn_piece(p):
        place = dn.at[rows_of(me * shard + p * DN_PIECE, DN_PIECE), :]
        return dn_shard.at[0, pl.ds(p * DN_PIECE, DN_PIECE), :], place, dn_recv.at[index * dn_pieces + p]

    shard_chunks = [gu_piece(p) for p in range(gu_pieces)] + [dn_piece(p) for p in range(dn_pieces)]

    @pl.when(target != me)
    def _():
        for source, place, sem in shard_chunks:
            pltpu.make_async_remote_copy(
                source, place, shard_send, sem, device_id=(target, z), device_id_type=MESH
            ).start()

    @pl.when(target == me)
    def _():
        for source, place, sem in shard_chunks:
            pltpu.make_async_copy(source, place, sem).start()

    mine = rows_of(q * SLOTS, SLOTS)

    def scatter_rows(source, place, send_sem, recv_sem):
        def step(k, carry):
            other = lax.rem(q + k, n)
            pltpu.make_async_remote_copy(
                source.at[rows_of(other * SLOTS, SLOTS), :],
                place.at[mine, :],
                send_sem,
                recv_sem,
                device_id=(2 * other + core, z),
                device_id_type=MESH,
            ).start()
            return carry

        pltpu.make_async_copy(source.at[mine, :], place.at[mine, :], recv_sem).start()
        lax.fori_loop(1, n, step, 0)

    def sent_rows(source, send_sem):
        rest = source.at[pl.ds(0, (n - 1) * SLOTS), :]
        pltpu.make_async_copy(rest, rest, send_sem).wait()

    def arrived_rows(place, recv_sem):
        pltpu.make_async_copy(place, place, recv_sem).wait()

    scatter_rows(send_t, in_t, row_send.at[0], row_recv.at[0])
    scatter_rows(send_g, in_g, row_send.at[1], row_recv.at[1])

    def pass_on(weight, start, size, recv_sem, sib_sem):
        chunk = weight.at[rows_of(start, size), :]
        pltpu.make_async_copy(chunk, chunk, recv_sem).wait()

        @pl.when(passes_on)
        def _():
            pltpu.make_async_remote_copy(
                chunk, chunk, ring_send, recv_sem, device_id=(me, after), device_id_type=MESH
            ).start()

        pltpu.make_async_remote_copy(
            chunk, chunk, sib_send, sib_sem, device_id=(sibling, z), device_id_type=MESH
        ).start()

    def gu_step(i, carry):
        p = i // sources
        s = i - p * sources
        start = core * half + s * shard + p * GU_PIECE
        pass_on(gu, start, GU_PIECE, gu_recv.at[i], sib_gu)
        return carry

    def dn_step(i, carry):
        pass_on(dn, core * half + i * DN_PIECE, DN_PIECE, dn_recv.at[i], sib_dn)
        return carry

    lax.fori_loop(0, gu_pieces * sources, gu_step, 0)
    lax.fori_loop(0, dn_pieces * sources, dn_step, 0)

    own = rows_of(core * half, half)
    theirs = rows_of((1 - core) * half, half)

    def wait_half(weight, sem, part):
        pltpu.make_async_copy(weight.at[part, :], weight.at[part, :], sem).wait()

    wait_half(gu, sib_gu, theirs)
    arrived_rows(in_t, row_recv.at[0])
    tile = min(256, ff)

    def gate_up_step(j, carry):
        cols = rows_of(j * tile, tile)
        gate[:, cols] = dot(in_t[...], gu[:, cols])
        up[:, cols] = dot(in_t[...], gu[:, rows_of(ff + j * tile, tile)])
        hidden[:, cols] = (jax.nn.silu(gate[:, cols]) * up[:, cols]).astype(jnp.bfloat16)
        return carry

    lax.fori_loop(0, ff // tile, gate_up_step, 0)
    wait_half(dn, sib_dn, theirs)

    def out_step(j, carry):
        cols = rows_of(j * tile, tile)
        out_s[:, cols] = dot_nt(hidden[...], dn[cols, :]).astype(jnp.bfloat16)
        return carry

    lax.fori_loop(0, width // tile, out_step, 0)
    scatter_rows(out_s, back_o, back_send.at[0], back_recv.at[0])

    arrived_rows(in_g, row_recv.at[1])

    def grad_hidden_step(j, carry):
        cols = rows_of(j * tile, tile)
        grad_hidden = dot(in_g[...], dn[:, cols])
        g = gate[:, cols]
        s = jax.nn.sigmoid(g)
        ggu[:, cols] = (grad_hidden * up[:, cols] * s * (1.0 + g * (1.0 - s))).astype(jnp.bfloat16)
        ggu[:, rows_of(ff + j * tile, tile)] = (grad_hidden * g * s).astype(jnp.bfloat16)
        return carry

    lax.fori_loop(0, ff // tile, grad_hidden_step, 0)

    def expert_grad_step(j, carry):
        cols = rows_of(j * tile, tile)
        eg_s[:, cols] = dot_nt(ggu[...], gu[cols, :]).astype(jnp.bfloat16)
        return carry

    lax.fori_loop(0, width // tile, expert_grad_step, 0)
    scatter_rows(eg_s, back_g, back_send.at[1], back_recv.at[1])

    @pl.when(passes_on)
    def _():
        wait_half(gu, ring_send, own)
        wait_half(dn, ring_send, own)

    wait_half(gu, sib_send, own)
    wait_half(dn, sib_send, own)

    @pl.when(target != me)
    def _():
        for weight in (gu, dn):
            part = weight.at[rows_of(me * shard, shard), :]
            pltpu.make_async_copy(part, part, shard_send).wait()

    sent_rows(send_t, row_send.at[0])
    sent_rows(send_g, row_send.at[1])

    first = weight_of.astype(jnp.bfloat16)
    rest = weight_of - first.astype(jnp.float32)
    second = rest.astype(jnp.bfloat16)
    third = (rest - second.astype(jnp.float32)).astype(jnp.bfloat16)
    chosen_half = chosen.astype(jnp.bfloat16)
    arrived_rows(back_o, back_recv.at[0])

    def mixed_step(j, products):
        cols = rows_of(j * tile, tile)
        out = back_o[:, cols]
        total = dot(first, out) + (dot(second, out) + dot(third, out))
        mixed[:, cols] = total.astype(jnp.bfloat16)
        return products + dot_nt(cotangent[:, cols], out)

    products = lax.fori_loop(
        0, width // tile, mixed_step, jnp.zeros((tok_rows, slots), jnp.float32)
    )
    products = jnp.where(kept, products, 0.0)
    for k in range(top):
        hit = routes[:, k : k + 1] == expert_of
        grad_gates[:, k : k + 1] = jnp.sum(jnp.where(hit, products, 0.0), axis=1, keepdims=True)

    arrived_rows(back_g, back_recv.at[1])

    def grad_step(j, carry):
        cols = rows_of(j * tile, tile)
        grad_tokens[:, cols] = dot(chosen_half, back_g[:, cols]).astype(jnp.bfloat16)
        return carry

    lax.fori_loop(0, width // tile, grad_step, 0)
    sent_rows(out_s, back_send.at[0])
    sent_rows(eg_s, back_send.at[1])


def on_device(tokens, cotangent, routes, route_weights, gate_up_weight, down_weight):
    n = lax.axis_size("expert")
    tok_rows, width = tokens.shape
    top = routes.shape[1]
    shard, ff = down_weight.shape[1:]
    capacity = 3 * tok_rows // 32
    slots = n * SLOTS
    rows = pltpu.VMEM((slots, width), jnp.bfloat16)
    gu_chunks = n * (shard // GU_PIECE)
    dn_chunks = n * (shard // DN_PIECE)
    dma = pltpu.SemaphoreType.DMA
    return pl.pallas_call(
        functools.partial(kernel, n, capacity),
        out_shape=(
            jax.ShapeDtypeStruct((tok_rows, width), jnp.bfloat16),
            jax.ShapeDtypeStruct((tok_rows, width), jnp.bfloat16),
            jax.ShapeDtypeStruct((tok_rows, top), jnp.float32),
        ),
        in_specs=[pl.BlockSpec(memory_space=pltpu.VMEM)] * 6,
        out_specs=[pl.BlockSpec(memory_space=pltpu.VMEM)] * 3,
        scratch_shapes=[
            pltpu.VMEM((width, 2 * ff), jnp.bfloat16),
            pltpu.VMEM((width, ff), jnp.bfloat16),
            rows,
            rows,
            rows,
            rows,
            pltpu.VMEM((slots, ff), jnp.float32),
            pltpu.VMEM((slots, ff), jnp.float32),
            pltpu.VMEM((slots, ff), jnp.bfloat16),
            pltpu.VMEM((slots, 2 * ff), jnp.bfloat16),
            rows,
            rows,
            rows,
            rows,
            dma((gu_chunks,)),
            dma((dn_chunks,)),
            dma,
            dma,
            dma,
            dma,
            dma,
            dma((2,)),
            dma((2,)),
            dma((2,)),
            dma((2,)),
        ],
        compiler_params=pltpu.CompilerParams(
            collective_id=0, has_side_effects=True, vmem_limit_bytes=44 * 1024 * 1024
        ),
    )(tokens, cotangent, routes, route_weights, gate_up_weight, down_weight)


def solution(mesh):
    rows = P(("fsdp", "expert"), None)
    weight = P("expert", "fsdp", None)
    return jax.shard_map(
        on_device,
        mesh=mesh,
        in_specs=(rows, rows, rows, rows, weight, weight),
        out_specs=(rows, rows, rows),
        check_vma=False,
    )
```

```python
import functools

import jax
import jax.numpy as jnp
from jax import lax
from jax.experimental import pallas as pl
from jax.experimental.pallas import tpu as pltpu
from jax.sharding import PartitionSpec as P

MESH = pl.DeviceIdType.MESH
SLOTS = 16
GU_PIECE = 16
DN_PIECE = 32
GU_CHUNKS = 64
CHUNKS = 3 * GU_CHUNKS
MEET_FIRST, MEET_STEP = 132, 5
GU_LEAD, DN_LEAD = 5, 20
HOP, SLACK = 6, 8
T_CALL, G_CALL = 70, 100
NT = (((1,), (1,)), ((), ()))


def dot(a, b):
    return jnp.dot(a, b, preferred_element_type=jnp.float32)


def dot_nt(a, b):
    return lax.dot_general(a, b, NT, preferred_element_type=jnp.float32)


def rows_of(start, size):
    return pl.ds(pl.multiple_of(start, size), size)


def nearest_row(q, h):
    y = q // 4
    a = lax.rem(2 * h - y + 4, 4)
    b = lax.rem(2 * h + 1 - y + 4, 4)
    return jnp.where(jnp.minimum(a, 4 - a) <= jnp.minimum(b, 4 - b), 2 * h, 2 * h + 1)


def device_at(q, h, near, j):
    k = j // 2
    row = jnp.where(k < 4, near, 4 * h + 1 - near)
    d = lax.rem(k, 4)
    x = lax.rem(lax.rem(q, 4) + d + jnp.where(d == 2, 1, 0) - jnp.where(d == 3, 1, 0), 4)
    return 2 * (4 * row + x) + lax.rem(j, 2)


def rank_of(q, f):
    c = f // 2
    near = nearest_row(q, c // 8)
    off = lax.rem(lax.rem(c, 4) - lax.rem(q, 4) + 4, 4)
    d = off - jnp.where(off == 3, 1, 0) + jnp.where(off == 2, 1, 0)
    return 2 * (jnp.where(c // 4 == near, 0, 4) + d) + lax.rem(f, 2)


def kernel(
    n,
    capacity,
    tokens_hbm,
    cotangent_hbm,
    routes,
    route_weights,
    gu_shard,
    dn_shard,
    mixed,
    grad_tokens,
    grad_gates,
    tokens,
    cotangent,
    gu,
    dn,
    send_t,
    send_g,
    in_t,
    in_g,
    gate,
    up,
    hidden,
    ggu,
    out_s,
    eg_s,
    back_o,
    back_g,
    load,
    ring,
    sib,
    ring_send,
    sib_send,
    shard_send,
    row_recv,
    row_send,
    back_recv,
    back_send,
    go,
):
    tok_rows, width = tokens.shape
    top = routes.shape[0]
    shard = gu_shard.shape[1]
    ff = dn_shard.shape[2]
    slots = n * SLOTS
    me = lax.axis_index("fsdp")
    z = lax.axis_index("expert")
    q = me // 2
    core = lax.rem(me, 2)
    sibling = me + 1 - 2 * core
    upward = core == 0
    after = lax.rem(z + 1 + core * (n - 2), n)
    before = lax.rem(z + n - 1 - core * (n - 2), n)

    loads = (
        pltpu.make_async_copy(tokens_hbm, tokens, load.at[0]),
        pltpu.make_async_copy(cotangent_hbm, cotangent, load.at[1]),
    )
    for copy in loads:
        copy.start()

    barrier = pltpu.get_barrier_semaphore()

    def greet(k, carry):
        pl.semaphore_signal(
            barrier, inc=1, device_id=(lax.rem(me + k, 2 * n), z), device_id_type=MESH
        )
        return carry

    pl.semaphore_signal(barrier, inc=1, device_id=(me, after), device_id_type=MESH)
    pl.semaphore_signal(barrier, inc=1, device_id=(me, before), device_id_type=MESH)
    lax.fori_loop(1, 2 * n, greet, 0)

    slot_id = lax.broadcasted_iota(jnp.int32, (slots, tok_rows), 0)
    expert_of = slot_id // SLOTS
    slot_of = slot_id - expert_of * SLOTS
    weight_of = jnp.zeros((slots, tok_rows), jnp.float32)
    named = jnp.zeros((slots, tok_rows), jnp.float32)
    for k in range(top):
        hit = routes[k : k + 1, :] == expert_of
        named = jnp.where(hit, 1.0, named)
        weight_of = jnp.where(hit, route_weights[k : k + 1, :], weight_of)
    row_id = lax.broadcasted_iota(jnp.int32, (tok_rows, tok_rows), 0)
    col_id = lax.broadcasted_iota(jnp.int32, (tok_rows, tok_rows), 1)
    above = jnp.where(row_id < col_id, 1.0, 0.0).astype(jnp.bfloat16)
    earlier = dot(named.astype(jnp.bfloat16), above).astype(jnp.int32)
    kept = (named > 0.5) & (earlier == slot_of) & (slot_of < capacity)
    chosen = jnp.where(kept, 1.0, 0.0)
    weight_of = jnp.where(kept, weight_of, 0.0)
    picks = chosen.astype(jnp.bfloat16)
    slot_weight = jnp.sum(weight_of, axis=1, keepdims=True)
    loads[0].wait()
    send_t[...] = dot(picks, tokens[...]).astype(jnp.bfloat16)
    loads[1].wait()
    send_g[...] = (slot_weight * dot(picks, cotangent[...])).astype(jnp.bfloat16)

    pl.semaphore_wait(barrier, 2 * n + 1)

    def meet(d):
        return jnp.minimum(jnp.maximum(8 * ((MEET_FIRST - MEET_STEP * d + 4) // 8), GU_CHUNKS), 2 * GU_CHUNKS)

    d = lax.rem(z - q + n, n)
    dist = jnp.where(upward, d, lax.rem(n - d, n))
    next_d = jnp.where(upward, d + 1, lax.rem(d + n - 1, n))
    is_first = d == 0
    own = jnp.where(is_first, CHUNKS // 2, jnp.where(upward, meet(d), CHUNKS - meet(d)))
    passed = jnp.where(upward, meet(next_d), CHUNKS - meet(next_d))
    passed = jnp.where((next_d == 0) | (next_d == n), 0, passed)

    def number(u):
        return jnp.where(upward, u, CHUNKS - 1 - u)

    half_me = q // (n // 2)
    target = 2 * z + half_me
    rank = rank_of(z, me)
    is_remote = target != me

    def place_in_order(t):
        return jnp.where(half_me == 0, t, CHUNKS - 1 - t)

    def gu_shard_chunks():
        for p in range(shard // GU_PIECE):
            yield (
                gu_shard.at[0, pl.ds(p * GU_PIECE, GU_PIECE), :],
                gu.at[rows_of(me * shard + p * GU_PIECE, GU_PIECE), :],
                ring.at[place_in_order(4 * rank + p)],
            )

    def dn_shard_chunks():
        for p in range(shard // DN_PIECE):
            yield (
                dn_shard.at[0, pl.ds(p * DN_PIECE, DN_PIECE), :],
                dn.at[rows_of(me * shard + p * DN_PIECE, DN_PIECE), :],
                ring.at[place_in_order(GU_CHUNKS + 2 * rank + p)],
            )

    def send_shard(chunks, k):
        for source, place, sem in chunks():
            pltpu.make_async_remote_copy(
                source, place, shard_send.at[k], sem, device_id=(target, z), device_id_type=MESH
            ).start()

    def send_shard_on_call(chunks, k):
        pl.semaphore_wait(go.at[k], 1)
        send_shard(chunks, k)

    at_once = rank < GU_LEAD
    gu_call = 4 * (rank - GU_LEAD) - HOP * dist + SLACK
    dn_call = GU_CHUNKS + 2 * rank - DN_LEAD - HOP * dist + SLACK

    @pl.when(jnp.logical_not(is_remote))
    def _():
        for chunks in (gu_shard_chunks, dn_shard_chunks):
            for source, place, sem in chunks():
                pltpu.make_async_copy(source, place, sem).start()

    @pl.when(is_remote & at_once)
    def _():
        send_shard(gu_shard_chunks, 0)

    @pl.when(is_remote & jnp.logical_not(at_once) & (gu_call < 0))
    def _():
        send_shard_on_call(gu_shard_chunks, 0)

    @pl.when(is_remote & (dn_call < 0))
    def _():
        send_shard_on_call(dn_shard_chunks, 1)

    gu_call = jnp.where(is_remote & jnp.logical_not(at_once), gu_call, -1)
    dn_call = jnp.where(is_remote, dn_call, -1)

    mine = rows_of(q * SLOTS, SLOTS)

    def scatter_rows(source, place, send_sem, recv_sem):
        def step(k, carry):
            other = lax.rem(q + k, n)
            pltpu.make_async_remote_copy(
                source.at[rows_of(other * SLOTS, SLOTS), :],
                place.at[mine, :],
                send_sem,
                recv_sem,
                device_id=(2 * other + core, z),
                device_id_type=MESH,
            ).start()
            return carry

        pltpu.make_async_copy(source.at[mine, :], place.at[mine, :], recv_sem).start()
        lax.fori_loop(1, n, step, 0)

    def sent_rows(source, send_sem):
        rest = source.at[pl.ds(0, (n - 1) * SLOTS), :]
        pltpu.make_async_copy(rest, rest, send_sem).wait()

    def arrived_rows(place, recv_sem):
        pltpu.make_async_copy(place, place, recv_sem).wait()

    t_call = jnp.maximum(T_CALL - HOP * dist, 0)
    g_call = jnp.minimum(jnp.maximum(G_CALL - HOP * dist, 1), own - 1)

    near = (nearest_row(q, 0), nearest_row(q, 1))

    def half_of(u):
        i = number(u)
        h = jnp.where(i < CHUNKS // 2, 0, 1)
        t = jnp.where(h == 0, i, CHUNKS - 1 - i)
        return h, t, jnp.where(h == 0, near[0], near[1])

    def gu_chunk(u):
        h, t, row = half_of(u)
        start = device_at(q, h, row, t // 4) * shard + lax.rem(t, 4) * GU_PIECE
        return gu.at[rows_of(start, GU_PIECE), :]

    def dn_chunk(u):
        h, t, row = half_of(u)
        t = t - GU_CHUNKS
        start = device_at(q, h, row, t // 2) * shard + lax.rem(t, 2) * DN_PIECE
        return dn.at[rows_of(start, DN_PIECE), :]

    def pass_on(chunk, u):
        i = number(u)

        @pl.when(u < passed)
        def _():
            pltpu.make_async_remote_copy(
                chunk, chunk, ring_send.at[i // 8], ring.at[i], device_id=(me, after), device_id_type=MESH
            ).start()

    def take(chunk, u):
        i = number(u)
        pltpu.make_async_copy(chunk, chunk, ring.at[i]).wait()
        pass_on(chunk, u)
        pltpu.make_async_remote_copy(
            chunk, chunk, sib_send.at[i // 8], sib.at[i // 8], device_id=(sibling, z), device_id_type=MESH
        ).start()

    def call_shards(u):
        def call(j, k):
            f = device_at(q, core, jnp.where(upward, near[0], near[1]), j)

            @pl.when(f != me)
            def _():
                pl.semaphore_signal(go.at[k], inc=1, device_id=(f, z), device_id_type=MESH)

        j = u // 4 + GU_LEAD
        k = (u - GU_CHUNKS + DN_LEAD) // 2

        @pl.when(is_first & (lax.rem(u, 4) == 0) & (j < n))
        def _():
            call(j, 0)

        @pl.when(is_first & (lax.rem(u, 2) == 0) & (u >= GU_CHUNKS - DN_LEAD) & (k < n))
        def _():
            call(k, 1)

    def beside(u):
        call_shards(u)

        @pl.when(u == gu_call)
        def _():
            send_shard_on_call(gu_shard_chunks, 0)

        @pl.when(u == dn_call)
        def _():
            send_shard_on_call(dn_shard_chunks, 1)

        @pl.when(u == t_call)
        def _():
            scatter_rows(send_t, in_t, row_send.at[0], row_recv.at[0])

        @pl.when(u == g_call)
        def _():
            scatter_rows(send_g, in_g, row_send.at[1], row_recv.at[1])

    def gu_step(u, carry):
        beside(u)
        take(gu_chunk(u), u)
        return carry

    def dn_step(u, carry):
        beside(u)
        take(dn_chunk(u), u)
        return carry

    lax.fori_loop(0, GU_CHUNKS, gu_step, 0)
    lax.fori_loop(GU_CHUNKS, own, dn_step, 0)

    def wait_group(g, sems):
        group = gu.at[pl.ds(0, 8 * GU_PIECE), :]
        pltpu.make_async_copy(group, group, sems.at[number(8 * g) // 8]).wait()

    def group_step(g, carry):
        wait_group(g, sib)

        def one(k, carry):
            pass_on(dn_chunk(8 * g + k), 8 * g + k)
            return carry

        lax.fori_loop(0, 8, one, 0)
        return carry

    def wait_step(g, carry):
        wait_group(g, sib)
        return carry

    seen = jnp.maximum(own, passed) // 8
    lax.fori_loop(own // 8, seen, group_step, 0)
    lax.fori_loop(2 * GU_CHUNKS // 8, CHUNKS // 8, wait_step, 0)

    arrived_rows(in_t, row_recv.at[0])
    tile = min(256, ff)

    def gate_up_step(j, carry):
        cols = rows_of(j * tile, tile)
        gate[:, cols] = dot(in_t[...], gu[:, cols])
        up[:, cols] = dot(in_t[...], gu[:, rows_of(ff + j * tile, tile)])
        hidden[:, cols] = (jax.nn.silu(gate[:, cols]) * up[:, cols]).astype(jnp.bfloat16)
        return carry

    lax.fori_loop(0, ff // tile, gate_up_step, 0)
    lax.fori_loop(seen, 2 * GU_CHUNKS // 8, wait_step, 0)

    def out_step(j, carry):
        cols = rows_of(j * tile, tile)
        out_s[:, cols] = dot_nt(hidden[...], dn[cols, :]).astype(jnp.bfloat16)
        return carry

    lax.fori_loop(0, width // tile, out_step, 0)
    scatter_rows(out_s, back_o, back_send.at[0], back_recv.at[0])

    arrived_rows(in_g, row_recv.at[1])

    def grad_hidden_step(j, carry):
        cols = rows_of(j * tile, tile)
        grad_hidden = dot(in_g[...], dn[:, cols])
        g = gate[:, cols]
        s = jax.nn.sigmoid(g)
        ggu[:, cols] = (grad_hidden * up[:, cols] * s * (1.0 + g * (1.0 - s))).astype(jnp.bfloat16)
        ggu[:, rows_of(ff + j * tile, tile)] = (grad_hidden * g * s).astype(jnp.bfloat16)
        return carry

    lax.fori_loop(0, ff // tile, grad_hidden_step, 0)

    def expert_grad_step(j, carry):
        cols = rows_of(j * tile, tile)
        eg_s[:, cols] = dot_nt(ggu[...], gu[cols, :]).astype(jnp.bfloat16)
        return carry

    lax.fori_loop(0, width // tile, expert_grad_step, 0)
    scatter_rows(eg_s, back_g, back_send.at[1], back_recv.at[1])

    def ring_sent(g, carry):
        wait_group(g, ring_send)
        return carry

    def sib_sent(g, carry):
        wait_group(g, sib_send)
        return carry

    lax.fori_loop(0, passed // 8, ring_sent, 0)
    lax.fori_loop(0, own // 8, sib_sent, 0)

    @pl.when(is_remote)
    def _():
        for k, weight in enumerate((gu, dn)):
            part = weight.at[rows_of(me * shard, shard), :]
            pltpu.make_async_copy(part, part, shard_send.at[k]).wait()

    sent_rows(send_t, row_send.at[0])
    sent_rows(send_g, row_send.at[1])

    by_token = jnp.transpose(weight_of)
    first = by_token.astype(jnp.bfloat16)
    rest = by_token - first.astype(jnp.float32)
    second = rest.astype(jnp.bfloat16)
    third = (rest - second.astype(jnp.float32)).astype(jnp.bfloat16)
    chosen_by_token = jnp.transpose(chosen).astype(jnp.bfloat16)
    arrived_rows(back_o, back_recv.at[0])

    def mixed_step(j, products):
        cols = rows_of(j * tile, tile)
        out = back_o[:, cols]
        total = dot(first, out) + (dot(second, out) + dot(third, out))
        mixed[:, cols] = total.astype(jnp.bfloat16)
        return products + dot_nt(out, cotangent[:, cols])

    products = lax.fori_loop(
        0, width // tile, mixed_step, jnp.zeros((slots, tok_rows), jnp.float32)
    )
    products = jnp.where(kept, products, 0.0)
    for k in range(top):
        hit = routes[k : k + 1, :] == expert_of
        grad_gates[k : k + 1, :] = jnp.sum(jnp.where(hit, products, 0.0), axis=0, keepdims=True)

    arrived_rows(back_g, back_recv.at[1])

    def grad_step(j, carry):
        cols = rows_of(j * tile, tile)
        grad_tokens[:, cols] = dot(chosen_by_token, back_g[:, cols]).astype(jnp.bfloat16)
        return carry

    lax.fori_loop(0, width // tile, grad_step, 0)
    sent_rows(out_s, back_send.at[0])
    sent_rows(eg_s, back_send.at[1])


def on_device(tokens, cotangent, routes, route_weights, gate_up_weight, down_weight):
    n = lax.axis_size("expert")
    tok_rows, width = tokens.shape
    top = routes.shape[1]
    shard, ff = down_weight.shape[1:]
    capacity = 3 * tok_rows // 32
    slots = n * SLOTS
    rows = pltpu.VMEM((slots, width), jnp.bfloat16)
    dma = pltpu.SemaphoreType.DMA
    hbm = pl.BlockSpec(memory_space=pl.ANY)
    vmem = pl.BlockSpec(memory_space=pltpu.VMEM)
    mixed, grad_tokens, grad_gates = pl.pallas_call(
        functools.partial(kernel, n, capacity),
        out_shape=(
            jax.ShapeDtypeStruct((tok_rows, width), jnp.bfloat16),
            jax.ShapeDtypeStruct((tok_rows, width), jnp.bfloat16),
            jax.ShapeDtypeStruct((top, tok_rows), jnp.float32),
        ),
        in_specs=[hbm, hbm, vmem, vmem, hbm, hbm],
        out_specs=[vmem] * 3,
        scratch_shapes=[
            pltpu.VMEM((tok_rows, width), jnp.bfloat16),
            pltpu.VMEM((tok_rows, width), jnp.bfloat16),
            pltpu.VMEM((width, 2 * ff), jnp.bfloat16),
            pltpu.VMEM((width, ff), jnp.bfloat16),
            rows,
            rows,
            rows,
            rows,
            pltpu.VMEM((slots, ff), jnp.float32),
            pltpu.VMEM((slots, ff), jnp.float32),
            pltpu.VMEM((slots, ff), jnp.bfloat16),
            pltpu.VMEM((slots, 2 * ff), jnp.bfloat16),
            rows,
            rows,
            rows,
            rows,
            dma((2,)),
            dma((CHUNKS,)),
            dma((CHUNKS // 8,)),
            dma((CHUNKS // 8,)),
            dma((CHUNKS // 8,)),
            dma((2,)),
            dma((2,)),
            dma((2,)),
            dma((2,)),
            dma((2,)),
            pltpu.SemaphoreType.REGULAR((2,)),
        ],
        compiler_params=pltpu.CompilerParams(
            collective_id=0, has_side_effects=True, vmem_limit_bytes=56 * 1024 * 1024
        ),
    )(tokens, cotangent, routes.T, route_weights.T, gate_up_weight, down_weight)
    return mixed, grad_tokens, grad_gates.T


def solution(mesh):
    rows = P(("fsdp", "expert"), None)
    weight = P("expert", "fsdp", None)
    return jax.shard_map(
        on_device,
        mesh=mesh,
        in_specs=(rows, rows, rows, rows, weight, weight),
        out_specs=(rows, rows, rows),
        check_vma=False,
    )
```

```python
import functools

import jax
import jax.numpy as jnp
from jax import lax
from jax.experimental import pallas as pl
from jax.experimental.pallas import tpu as pltpu
from jax.sharding import PartitionSpec as P

MESH = pl.DeviceIdType.MESH
SLOTS = 16
GU_PIECE = 16
DN_PIECE = 32
GU_CHUNKS = 64
CHUNKS = 3 * GU_CHUNKS
MEET_FIRST, MEET_STEP = 130, 5
GU_LEAD, DN_LEAD = 5, 20
HOP, SLACK = 6, 8
ROW_CALL, ROW_EVERY = 110, 2
OTHER_UP, OTHER_DOWN, OTHER_STEP = 77, 98, 11
MARGIN = 10
WIDE = 512
NT = (((1,), (1,)), ((), ()))


def dot(a, b):
    return jnp.dot(a, b, preferred_element_type=jnp.float32)


def dot_nt(a, b):
    return lax.dot_general(a, b, NT, preferred_element_type=jnp.float32)


def rows_of(start, size):
    return pl.ds(pl.multiple_of(start, size), size)


def nearest_row(q, h):
    y = q // 4
    a = lax.rem(2 * h - y + 4, 4)
    b = lax.rem(2 * h + 1 - y + 4, 4)
    return jnp.where(jnp.minimum(a, 4 - a) <= jnp.minimum(b, 4 - b), 2 * h, 2 * h + 1)


def chip_at(q, r):
    k = r // 2
    h = jnp.where(lax.rem(r, 2) == 0, q // 8, 1 - q // 8)
    near = nearest_row(q, h)
    row = jnp.where(k < 4, near, 4 * h + 1 - near)
    d = lax.rem(k, 4)
    x = lax.rem(lax.rem(q, 4) + d + jnp.where(d == 2, 1, 0) - jnp.where(d == 3, 1, 0), 4)
    return 4 * row + x


def rank_of(q, c):
    near = nearest_row(q, c // 8)
    off = lax.rem(lax.rem(c, 4) - lax.rem(q, 4) + 4, 4)
    d = off - jnp.where(off == 3, 1, 0) + jnp.where(off == 2, 1, 0)
    return 2 * (jnp.where(c // 4 == near, 0, 4) + d) + jnp.where(c // 8 == q // 8, 0, 1)


def is_opposite(q, c):
    return (lax.rem(c // 4 - q // 4 + 4, 4) == 2) & (lax.rem(c, 4) != lax.rem(q, 4))


def kernel(
    n,
    capacity,
    tokens_hbm,
    cotangent_hbm,
    routes,
    route_weights,
    gu_shard,
    dn_shard,
    mixed,
    back_g,
    by_slot,
    grad_gates,
    tokens,
    cotangent,
    gu,
    dn,
    send_t,
    send_g,
    in_t,
    in_g,
    gate,
    up,
    hidden,
    ggu,
    out_s,
    eg_s,
    back_o,
    gu_other,
    dn_other,
    load,
    ring,
    sib,
    ring_send,
    sib_send,
    shard_send,
    row_recv,
    row_send,
    back_recv,
    back_send,
    other_recv,
    go,
):
    tok_rows, width = tokens.shape
    top = routes.shape[0]
    shard = gu_shard.shape[1]
    ff = dn_shard.shape[2]
    slots = n * SLOTS
    me = lax.axis_index("fsdp")
    z = lax.axis_index("expert")
    q = me // 2
    core = lax.rem(me, 2)
    sibling = me + 1 - 2 * core
    upward = core == 0
    after = lax.rem(z + 1 + core * (n - 2), n)
    before = lax.rem(z + n - 1 - core * (n - 2), n)

    loads = (
        pltpu.make_async_copy(tokens_hbm, tokens, load.at[0]),
        pltpu.make_async_copy(cotangent_hbm, cotangent, load.at[1]),
    )
    for copy in loads:
        copy.start()

    barrier = pltpu.get_barrier_semaphore()

    def greet(k, carry):
        pl.semaphore_signal(
            barrier, inc=1, device_id=(lax.rem(me + k, 2 * n), z), device_id_type=MESH
        )
        return carry

    pl.semaphore_signal(barrier, inc=1, device_id=(me, after), device_id_type=MESH)
    pl.semaphore_signal(barrier, inc=1, device_id=(me, before), device_id_type=MESH)
    lax.fori_loop(1, 2 * n, greet, 0)

    slot_id = lax.broadcasted_iota(jnp.int32, (slots, tok_rows), 0)
    expert_of = slot_id // SLOTS
    slot_of = slot_id - expert_of * SLOTS
    weight_of = jnp.zeros((slots, tok_rows), jnp.float32)
    named = jnp.zeros((slots, tok_rows), jnp.float32)
    for k in range(top):
        hit = routes[k : k + 1, :] == expert_of
        named = jnp.where(hit, 1.0, named)
        weight_of = jnp.where(hit, route_weights[k : k + 1, :], weight_of)
    row_id = lax.broadcasted_iota(jnp.int32, (tok_rows, tok_rows), 0)
    col_id = lax.broadcasted_iota(jnp.int32, (tok_rows, tok_rows), 1)
    above = jnp.where(row_id < col_id, 1.0, 0.0).astype(jnp.bfloat16)
    earlier = dot(named.astype(jnp.bfloat16), above).astype(jnp.int32)
    kept = (named > 0.5) & (earlier == slot_of) & (slot_of < capacity)
    chosen = jnp.where(kept, 1.0, 0.0)
    weight_of = jnp.where(kept, weight_of, 0.0)
    picks = chosen.astype(jnp.bfloat16)
    slot_weight = jnp.sum(weight_of, axis=1, keepdims=True)
    loads[0].wait()
    send_t[...] = dot(picks, tokens[...]).astype(jnp.bfloat16)
    loads[1].wait()
    send_g[...] = (slot_weight * dot(picks, cotangent[...])).astype(jnp.bfloat16)

    pl.semaphore_wait(barrier, 2 * n + 1)

    def meet(d):
        return jnp.minimum(jnp.maximum(8 * ((MEET_FIRST - MEET_STEP * d + 4) // 8), GU_CHUNKS), 2 * GU_CHUNKS)

    d = lax.rem(z - q + n, n)
    dist = jnp.where(upward, d, lax.rem(n - d, n))
    next_d = jnp.where(upward, d + 1, lax.rem(d + n - 1, n))
    is_first = d == 0
    own = jnp.where(is_first, CHUNKS // 2, jnp.where(upward, meet(d), CHUNKS - meet(d)))
    passed = jnp.where(upward, meet(next_d), CHUNKS - meet(next_d))
    passed = jnp.where((next_d == 0) | (next_d == n), 0, passed)

    def number(u):
        return jnp.where(upward, u, CHUNKS - 1 - u)

    is_target = q == z
    opposite = lax.rem(q + n // 2, n)
    goes_by = is_opposite(z, q)
    is_between = is_opposite(z, opposite)
    between = 4 * (z // 4) + lax.rem(q, 4)

    def place_in_order(t):
        return jnp.where(upward, t, CHUNKS - 1 - t)

    def shard_chunks(part, source, chip):
        owner, rank = 2 * chip + core, rank_of(z, chip)
        size, weight, at = ((GU_PIECE, gu, 4 * rank), (DN_PIECE, dn, GU_CHUNKS + 2 * rank))[part]
        for p in range(shard // size):
            yield (
                source.at[pl.ds(p * size, size), :],
                weight.at[rows_of(owner * shard + p * size, size), :],
                ring.at[place_in_order(at + p)],
            )

    shards = (gu_shard.at[0], dn_shard.at[0])
    others = (gu_other, dn_other)

    def send_shard(part):
        for source, place, sem in shard_chunks(part, shards[part], q):
            pltpu.make_async_remote_copy(
                source, place, shard_send.at[part], sem, device_id=(2 * z + core, z), device_id_type=MESH
            ).start()

    def send_shard_on_call(part):
        pl.semaphore_wait(go.at[part], 1)
        send_shard(part)

    def send_other_on_call(part):
        pltpu.make_async_copy(others[part], others[part], other_recv.at[part]).wait()
        pl.semaphore_wait(go.at[2 + part], 1)
        for source, place, sem in shard_chunks(part, others[part], opposite):
            pltpu.make_async_remote_copy(
                source, place, shard_send.at[2 + part], sem, device_id=(2 * z + core, z), device_id_type=MESH
            ).start()

    def calls(rank):
        gu_call = 4 * (rank - GU_LEAD) - HOP * dist + SLACK
        dn_call = GU_CHUNKS + 2 * rank - DN_LEAD - HOP * dist + SLACK
        return gu_call, dn_call

    rank = rank_of(z, q)
    at_once = rank < GU_LEAD
    is_direct = jnp.logical_not(is_target | goes_by)
    gu_call, dn_call = calls(rank)
    gu_other_call, dn_other_call = calls(rank_of(z, opposite))

    @pl.when(is_target)
    def _():
        for part in range(2):
            for source, place, sem in shard_chunks(part, shards[part], q):
                pltpu.make_async_copy(source, place, sem).start()

    @pl.when(goes_by)
    def _():
        for part in range(2):
            pltpu.make_async_remote_copy(
                shards[part],
                others[part],
                shard_send.at[part],
                other_recv.at[part],
                device_id=(2 * between + core, z),
                device_id_type=MESH,
            ).start()

    @pl.when(is_direct & at_once)
    def _():
        send_shard(0)

    @pl.when(is_direct & jnp.logical_not(at_once) & (gu_call < 0))
    def _():
        send_shard_on_call(0)

    @pl.when(is_between & (gu_other_call < 0))
    def _():
        send_other_on_call(0)

    @pl.when(is_direct & (dn_call < 0))
    def _():
        send_shard_on_call(1)

    @pl.when(is_between & (dn_other_call < 0))
    def _():
        send_other_on_call(1)

    gu_call = jnp.where(is_direct & jnp.logical_not(at_once), gu_call, -1)
    dn_call = jnp.where(is_direct, dn_call, -1)
    gu_other_call = jnp.where(is_between, gu_other_call, -1)
    dn_other_call = jnp.where(is_between, dn_other_call, -1)

    mine = rows_of(q * SLOTS, SLOTS)

    def keep_rows(source, place, recv_sem):
        pltpu.make_async_copy(source.at[mine, :], place.at[mine, :], recv_sem).start()

    def send_rows(k, source, place, send_sem, recv_sem):
        other = lax.rem(q + k, n)
        pltpu.make_async_remote_copy(
            source.at[rows_of(other * SLOTS, SLOTS), :],
            place.at[mine, :],
            send_sem,
            recv_sem,
            device_id=(2 * other + core, z),
            device_id_type=MESH,
        ).start()

    def scatter_rows(source, place, send_sem, recv_sem):
        def step(k, carry):
            send_rows(k, source, place, send_sem, recv_sem)
            return carry

        keep_rows(source, place, recv_sem)
        lax.fori_loop(1, n, step, 0)

    def sent_rows(source, send_sem):
        rest = source.at[pl.ds(0, (n - 1) * SLOTS), :]
        pltpu.make_async_copy(rest, rest, send_sem).wait()

    def arrived_rows(place, recv_sem):
        pltpu.make_async_copy(place, place, recv_sem).wait()

    keep_rows(send_t, in_t, row_recv.at[0])
    keep_rows(send_g, in_g, row_recv.at[1])
    row_call = jnp.minimum(jnp.maximum(ROW_CALL - HOP * dist, 0), own - 2 * ROW_EVERY * (n - 1))

    def gu_chunk(u):
        i = number(u)
        h = jnp.where(i < CHUNKS // 2, 0, 1)
        t = jnp.where(h == 0, i, CHUNKS - 1 - i)
        start = (2 * chip_at(q, t // 4) + h) * shard + lax.rem(t, 4) * GU_PIECE
        return gu.at[rows_of(start, GU_PIECE), :]

    def dn_chunk(u):
        i = number(u)
        h = jnp.where(i < CHUNKS // 2, 0, 1)
        t = jnp.where(h == 0, i, CHUNKS - 1 - i) - GU_CHUNKS
        start = (2 * chip_at(q, t // 2) + h) * shard + lax.rem(t, 2) * DN_PIECE
        return dn.at[rows_of(start, DN_PIECE), :]

    def pass_on(chunk, u):
        i = number(u)

        @pl.when(u < passed)
        def _():
            pltpu.make_async_remote_copy(
                chunk, chunk, ring_send.at[i // 8], ring.at[i], device_id=(me, after), device_id_type=MESH
            ).start()

    def take(chunk, u):
        i = number(u)
        pltpu.make_async_copy(chunk, chunk, ring.at[i]).wait()
        pass_on(chunk, u)
        pltpu.make_async_remote_copy(
            chunk, chunk, sib_send.at[i // 8], sib.at[i // 8], device_id=(sibling, z), device_id_type=MESH
        ).start()

    def call_shards(u):
        def call(r, part):
            chip = chip_at(q, r)
            by = is_opposite(q, chip)
            holder = jnp.where(by, 4 * (q // 4) + lax.rem(chip, 4), chip)

            @pl.when(chip != q)
            def _():
                pl.semaphore_signal(
                    go.at[jnp.where(by, 2 + part, part)],
                    inc=1,
                    device_id=(2 * holder + core, z),
                    device_id_type=MESH,
                )

        j = u // 4 + GU_LEAD
        k = (u - GU_CHUNKS + DN_LEAD) // 2

        @pl.when(is_first & (lax.rem(u, 4) == 0) & (j < n))
        def _():
            call(j, 0)

        @pl.when(is_first & (lax.rem(u, 2) == 0) & (u >= GU_CHUNKS - DN_LEAD) & (k < n))
        def _():
            call(k, 1)

    def beside(u):
        call_shards(u)

        @pl.when(u == gu_call)
        def _():
            send_shard_on_call(0)

        @pl.when(u == dn_call)
        def _():
            send_shard_on_call(1)

        @pl.when(u == gu_other_call)
        def _():
            send_other_on_call(0)

        @pl.when(u == dn_other_call)
        def _():
            send_other_on_call(1)

        k = (u - row_call) // ROW_EVERY

        @pl.when((u >= row_call) & (lax.rem(u - row_call, ROW_EVERY) == 0))
        def _():
            @pl.when(k < n - 1)
            def _():
                send_rows(k + 1, send_t, in_t, row_send.at[0], row_recv.at[0])

            @pl.when((k >= n - 1) & (k < 2 * (n - 1)))
            def _():
                send_rows(k - n + 2, send_g, in_g, row_send.at[1], row_recv.at[1])

    def wait_group(g, sems):
        group = gu.at[pl.ds(0, 8 * GU_PIECE), :]
        pltpu.make_async_copy(group, group, sems.at[number(8 * g) // 8]).wait()

    def wait_step(g, carry):
        wait_group(g, sib)
        return carry

    tile = min(256, ff)

    def wait_gate_up():
        lax.fori_loop(2 * GU_CHUNKS // 8, CHUNKS // 8, wait_step, 0)
        arrived_rows(in_t, row_recv.at[0])

    def gate_up(j):
        cols = rows_of(j * tile, tile)
        gate[:, cols] = dot(in_t[...], gu[:, cols])
        up[:, cols] = dot(in_t[...], gu[:, rows_of(ff + j * tile, tile)])
        hidden[:, cols] = (jax.nn.silu(gate[:, cols]) * up[:, cols]).astype(jnp.bfloat16)

    other_late = jnp.where(upward, OTHER_UP - OTHER_STEP * dist, OTHER_DOWN - OTHER_STEP * dist)
    gate_up_at = GU_CHUNKS + jnp.maximum(other_late, 0) + MARGIN
    is_early = (gate_up_at + 2 * (ff // tile) < own) & jnp.logical_not(is_first)
    gate_up_at = jnp.where(is_early, gate_up_at, CHUNKS)

    def gu_step(u, carry):
        beside(u)
        take(gu_chunk(u), u)
        return carry

    def dn_step(u, carry):
        beside(u)
        take(dn_chunk(u), u)
        j = (u - gate_up_at) // 2

        @pl.when(u == gate_up_at)
        def _():
            wait_gate_up()

        @pl.when((u >= gate_up_at) & (lax.rem(u - gate_up_at, 2) == 0) & (j < ff // tile))
        def _():
            gate_up(j)

        return carry

    lax.fori_loop(0, GU_CHUNKS, gu_step, 0)
    lax.fori_loop(GU_CHUNKS, own, dn_step, 0)

    def group_step(g, carry):
        wait_group(g, sib)

        def one(k, carry):
            pass_on(dn_chunk(8 * g + k), 8 * g + k)
            return carry

        lax.fori_loop(0, 8, one, 0)
        return carry

    seen = jnp.maximum(own, passed) // 8
    lax.fori_loop(own // 8, seen, group_step, 0)

    @pl.when(jnp.logical_not(is_early))
    def _():
        wait_gate_up()

        def gate_up_step(j, carry):
            gate_up(j)
            return carry

        lax.fori_loop(0, ff // tile, gate_up_step, 0)

    lax.fori_loop(seen, 2 * GU_CHUNKS // 8, wait_step, 0)

    kept_width = width * capacity // SLOTS
    parts = kept_width // WIDE
    row = lax.broadcasted_iota(jnp.int32, (slots, slots), 0)
    col = lax.broadcasted_iota(jnp.int32, (slots, slots), 1)

    def folds(row, col, part):
        r = row // SLOTS * SLOTS + (lax.rem(row, SLOTS) - capacity) * parts + part
        return jnp.where((lax.rem(row, SLOTS) >= capacity) & (col == r), 1.0, 0.0).astype(jnp.bfloat16)

    fold = [folds(row, col, part) for part in range(parts)]

    def packed(value, place):
        last = value(parts).astype(jnp.bfloat16)
        for part in range(parts):
            place[:, part * WIDE : (part + 1) * WIDE] = (value(part) + dot(fold[part], last)).astype(jnp.bfloat16)

    packed(lambda j: dot_nt(hidden[...], dn[j * WIDE : (j + 1) * WIDE, :]), out_s)
    scatter_rows(out_s, back_o, back_send.at[0], back_recv.at[0])

    arrived_rows(in_g, row_recv.at[1])

    def grad_hidden_step(j, carry):
        cols = rows_of(j * tile, tile)
        grad_hidden = dot(in_g[...], dn[:, cols])
        g = gate[:, cols]
        s = jax.nn.sigmoid(g)
        ggu[:, cols] = (grad_hidden * up[:, cols] * s * (1.0 + g * (1.0 - s))).astype(jnp.bfloat16)
        ggu[:, rows_of(ff + j * tile, tile)] = (grad_hidden * g * s).astype(jnp.bfloat16)
        return carry

    lax.fori_loop(0, ff // tile, grad_hidden_step, 0)
    packed(lambda j: dot_nt(ggu[...], gu[j * WIDE : (j + 1) * WIDE, :]), eg_s)
    scatter_rows(eg_s, back_g, back_send.at[1], back_recv.at[1])

    by_token = jnp.transpose(weight_of)
    first = by_token.astype(jnp.bfloat16)
    rest = by_token - first.astype(jnp.float32)
    second = rest.astype(jnp.bfloat16)
    third = (rest - second.astype(jnp.float32)).astype(jnp.bfloat16)
    by_slot[...] = jnp.transpose(chosen).astype(jnp.bfloat16)
    arrived_rows(back_o, back_recv.at[0])
    unfold = [folds(col, row, part) for part in range(parts)]
    last = sum(dot(unfold[part], back_o[:, part * WIDE : (part + 1) * WIDE]) for part in range(parts))
    products = jnp.zeros((slots, tok_rows), jnp.float32)
    for part in range(parts + 1):
        cols = slice(part * WIDE, (part + 1) * WIDE)
        out = back_o[:, cols] if part < parts else last.astype(jnp.bfloat16)
        mixed[:, cols] = (dot(first, out) + (dot(second, out) + dot(third, out))).astype(jnp.bfloat16)
        products = products + dot_nt(out, cotangent[:, cols])
    products = jnp.where(kept, products, 0.0)
    for k in range(top):
        hit = routes[k : k + 1, :] == expert_of
        grad_gates[k : k + 1, :] = jnp.sum(jnp.where(hit, products, 0.0), axis=0, keepdims=True)

    def ring_sent(g, carry):
        wait_group(g, ring_send)
        return carry

    def sib_sent(g, carry):
        wait_group(g, sib_send)
        return carry

    lax.fori_loop(0, passed // 8, ring_sent, 0)
    lax.fori_loop(0, own // 8, sib_sent, 0)

    @pl.when(jnp.logical_not(is_target))
    def _():
        for part in range(2):
            pltpu.make_async_copy(others[part], others[part], shard_send.at[part]).wait()

    @pl.when(is_between)
    def _():
        for part in range(2):
            pltpu.make_async_copy(others[part], others[part], shard_send.at[2 + part]).wait()

    sent_rows(send_t, row_send.at[0])
    sent_rows(send_g, row_send.at[1])
    sent_rows(out_s, back_send.at[0])
    sent_rows(eg_s, back_send.at[1])
    arrived_rows(back_g, back_recv.at[1])


def finish(capacity, mixed, back, by_slot, mixed_out, grad_out, grad, sems):
    slots, kept_width = back.shape
    parts = kept_width // WIDE
    copy_mixed = pltpu.make_async_copy(mixed, mixed_out, sems.at[0])
    copy_mixed.start()
    row = lax.broadcasted_iota(jnp.int32, (slots, slots), 0)
    col = lax.broadcasted_iota(jnp.int32, (slots, slots), 1)
    block = col // SLOTS * SLOTS
    copies = [copy_mixed]
    last = jnp.zeros((slots, WIDE), jnp.float32)
    for part in range(parts + 1):
        cols = slice(part * WIDE, (part + 1) * WIDE)
        if part < parts:
            rows = back[:, cols]
            source = block + (lax.rem(col, SLOTS) - capacity) * parts + part
            unfold = jnp.where((lax.rem(col, SLOTS) >= capacity) & (row == source), 1.0, 0.0)
            last = last + dot(unfold.astype(jnp.bfloat16), rows)
        else:
            rows = last.astype(jnp.bfloat16)
        grad[:, cols] = dot(by_slot[...], rows).astype(jnp.bfloat16)
        copy = pltpu.make_async_copy(grad.at[:, cols], grad_out.at[:, cols], sems.at[part + 1])
        copy.start()
        copies.append(copy)
    for copy in copies:
        copy.wait()


def on_device(tokens, cotangent, routes, route_weights, gate_up_weight, down_weight):
    n = lax.axis_size("expert")
    tok_rows, width = tokens.shape
    top = routes.shape[1]
    shard, ff = down_weight.shape[1:]
    capacity = 3 * tok_rows // 32
    slots = n * SLOTS
    rows = pltpu.VMEM((slots, width), jnp.bfloat16)
    dma = pltpu.SemaphoreType.DMA
    hbm = pl.BlockSpec(memory_space=pltpu.HBM)
    vmem = pl.BlockSpec(memory_space=pltpu.VMEM)
    kept_width = width * capacity // SLOTS
    packed_rows = pltpu.VMEM((slots, kept_width), jnp.bfloat16)
    mixed, back, by_slot, grad_gates = pl.pallas_call(
        functools.partial(kernel, n, capacity),
        out_shape=(
            jax.ShapeDtypeStruct((tok_rows, width), jnp.bfloat16),
            jax.ShapeDtypeStruct((slots, kept_width), jnp.bfloat16),
            jax.ShapeDtypeStruct((tok_rows, slots), jnp.bfloat16),
            jax.ShapeDtypeStruct((top, tok_rows), jnp.float32),
        ),
        in_specs=[hbm, hbm, vmem, vmem, hbm, hbm],
        out_specs=[vmem] * 4,
        scratch_shapes=[
            pltpu.VMEM((tok_rows, width), jnp.bfloat16),
            pltpu.VMEM((tok_rows, width), jnp.bfloat16),
            pltpu.VMEM((width, 2 * ff), jnp.bfloat16),
            pltpu.VMEM((width, ff), jnp.bfloat16),
            rows,
            rows,
            rows,
            rows,
            pltpu.VMEM((slots, ff), jnp.float32),
            pltpu.VMEM((slots, ff), jnp.float32),
            pltpu.VMEM((slots, ff), jnp.bfloat16),
            pltpu.VMEM((slots, 2 * ff), jnp.bfloat16),
            packed_rows,
            packed_rows,
            packed_rows,
            pltpu.VMEM((shard, 2 * ff), jnp.bfloat16),
            pltpu.VMEM((shard, ff), jnp.bfloat16),
            dma((2,)),
            dma((CHUNKS,)),
            dma((CHUNKS // 8,)),
            dma((CHUNKS // 8,)),
            dma((CHUNKS // 8,)),
            dma((4,)),
            dma((2,)),
            dma((2,)),
            dma((2,)),
            dma((2,)),
            dma((2,)),
            pltpu.SemaphoreType.REGULAR((4,)),
        ],
        compiler_params=pltpu.CompilerParams(
            collective_id=0, has_side_effects=True, vmem_limit_bytes=28 * 1024 * 1024
        ),
    )(tokens, cotangent, routes.T, route_weights.T, gate_up_weight, down_weight)
    mixed, grad_tokens = pl.pallas_call(
        functools.partial(finish, capacity),
        out_shape=(
            jax.ShapeDtypeStruct((tok_rows, width), jnp.bfloat16),
            jax.ShapeDtypeStruct((tok_rows, width), jnp.bfloat16),
        ),
        in_specs=[vmem] * 3,
        out_specs=[hbm] * 2,
        scratch_shapes=[
            pltpu.VMEM((tok_rows, width), jnp.bfloat16),
            dma((2 + kept_width // WIDE,)),
        ],
        compiler_params=pltpu.CompilerParams(vmem_limit_bytes=16 * 1024 * 1024),
    )(mixed, back, by_slot)
    return mixed, grad_tokens, grad_gates.T


def solution(mesh):
    rows = P(("fsdp", "expert"), None)
    weight = P("expert", "fsdp", None)
    return jax.shard_map(
        on_device,
        mesh=mesh,
        in_specs=(rows, rows, rows, rows, weight, weight),
        out_specs=(rows, rows, rows),
        check_vma=False,
    )
```

```python
import functools

import jax
import jax.numpy as jnp
from jax import lax
from jax.experimental import pallas as pl
from jax.experimental.pallas import tpu as pltpu
from jax.sharding import PartitionSpec as P

MESH = pl.DeviceIdType.MESH
SLOTS = 16
GU_PIECE = 16
DN_PIECE = 32
GU_CHUNKS = 64
CHUNKS = 3 * GU_CHUNKS
MEET_FIRST, MEET_STEP = 130, 5
AT_ONCE, GU_LEAD, DN_LEAD = 7, 7, 20
HOP, SLACK = 6, 8
ROW_CALL, ROW_EVERY = 110, 2
OTHER_UP, OTHER_DOWN, OTHER_STEP = 77, 98, 11
MARGIN = 10
WIDE = 512
FAR_FIRST = sorted(
    ((k % 4, k // 4) for k in range(1, 16)),
    key=lambda step: -sum(min(a, 4 - a) for a in step),
)
NT = (((1,), (1,)), ((), ()))


def dot(a, b):
    return jnp.dot(a, b, preferred_element_type=jnp.float32)


def dot_nt(a, b):
    return lax.dot_general(a, b, NT, preferred_element_type=jnp.float32)


def rows_of(start, size):
    return pl.ds(pl.multiple_of(start, size), size)


def nearest_row(q, h):
    y = q // 4
    a = lax.rem(2 * h - y + 4, 4)
    b = lax.rem(2 * h + 1 - y + 4, 4)
    return jnp.where(jnp.minimum(a, 4 - a) <= jnp.minimum(b, 4 - b), 2 * h, 2 * h + 1)


def chip_at(q, r):
    m = r // 3
    turn = r - 3 * m
    beyond = (turn == 2) | ((turn == 0) & (m >= 3))
    k_beyond = jnp.where(turn == 2, m, m + 2)
    k_near = jnp.where(turn == 1, jnp.where(m == 0, 1, m + 3), m + jnp.where(m > 0, 1, 0))
    k = jnp.where(beyond, k_beyond, k_near)
    h = jnp.where(beyond, 1 - q // 8, q // 8)
    near = nearest_row(q, h)
    row = jnp.where(k < 4, near, 4 * h + 1 - near)
    d = lax.rem(k, 4)
    x = lax.rem(lax.rem(q, 4) + d + jnp.where(d == 2, 1, 0) - jnp.where(d == 3, 1, 0), 4)
    return 4 * row + x


def rank_of(q, c):
    near = nearest_row(q, c // 8)
    off = lax.rem(lax.rem(c, 4) - lax.rem(q, 4) + 4, 4)
    d = off - jnp.where(off == 3, 1, 0) + jnp.where(off == 2, 1, 0)
    k = jnp.where(c // 4 == near, 0, 4) + d
    of_near = jnp.where(k < 2, k, jnp.where(k < 4, 3 * k - 3, 3 * k - 8))
    of_beyond = jnp.where(k < 5, 3 * k + 2, 3 * k - 6)
    return jnp.where(c // 8 == q // 8, of_near, of_beyond)


def is_opposite(q, c):
    return (lax.rem(c // 4 - q // 4 + 4, 4) == 2) & (lax.rem(c, 4) != lax.rem(q, 4))


def kernel(
    n,
    capacity,
    tokens_hbm,
    cotangent_hbm,
    routes,
    route_weights,
    gu_shard,
    dn_shard,
    mixed,
    back_g,
    by_slot,
    grad_gates,
    tokens,
    cotangent,
    gu,
    dn,
    send_t,
    send_g,
    in_t,
    in_g,
    gate,
    up,
    hidden,
    ggu,
    out_s,
    eg_s,
    back_o,
    gu_other,
    dn_other,
    load,
    ring,
    sib,
    ring_send,
    sib_send,
    shard_send,
    row_recv,
    row_send,
    back_recv,
    back_send,
    other_recv,
    go,
):
    tok_rows, width = tokens.shape
    top = routes.shape[0]
    shard = gu_shard.shape[1]
    ff = dn_shard.shape[2]
    slots = n * SLOTS
    me = lax.axis_index("fsdp")
    z = lax.axis_index("expert")
    q = me // 2
    core = lax.rem(me, 2)
    sibling = me + 1 - 2 * core
    upward = core == 0
    after = lax.rem(z + 1 + core * (n - 2), n)
    before = lax.rem(z + n - 1 - core * (n - 2), n)

    loads = (
        pltpu.make_async_copy(tokens_hbm, tokens, load.at[0]),
        pltpu.make_async_copy(cotangent_hbm, cotangent, load.at[1]),
    )
    for copy in loads:
        copy.start()

    barrier = pltpu.get_barrier_semaphore()

    def greet(k, carry):
        other = 2 * lax.rem(q + k, n) + core
        pl.semaphore_signal(barrier, inc=1, device_id=(other, z), device_id_type=MESH)
        return carry

    pl.semaphore_signal(barrier, inc=1, device_id=(me, after), device_id_type=MESH)
    pl.semaphore_signal(barrier, inc=1, device_id=(me, before), device_id_type=MESH)
    pl.semaphore_signal(barrier, inc=1, device_id=(sibling, z), device_id_type=MESH)
    lax.fori_loop(1, n, greet, 0)

    pl.semaphore_wait(barrier, n + 2)

    def meet(d):
        return jnp.minimum(jnp.maximum(8 * ((MEET_FIRST - MEET_STEP * d + 4) // 8), GU_CHUNKS), 2 * GU_CHUNKS)

    d = lax.rem(z - q + n, n)
    dist = jnp.where(upward, d, lax.rem(n - d, n))
    next_d = jnp.where(upward, d + 1, lax.rem(d + n - 1, n))
    is_first = d == 0
    own = jnp.where(is_first, CHUNKS // 2, jnp.where(upward, meet(d), CHUNKS - meet(d)))
    passed = jnp.where(upward, meet(next_d), CHUNKS - meet(next_d))
    passed = jnp.where((next_d == 0) | (next_d == n), 0, passed)

    def number(u):
        return jnp.where(upward, u, CHUNKS - 1 - u)

    is_target = q == z
    opposite = lax.rem(q + n // 2, n)
    goes_by = is_opposite(z, q)
    is_between = is_opposite(z, opposite)
    between = 4 * (z // 4) + lax.rem(q, 4)

    def place_in_order(t):
        return jnp.where(upward, t, CHUNKS - 1 - t)

    def shard_chunks(part, source, chip):
        owner, rank = 2 * chip + core, rank_of(z, chip)
        size, weight, at = ((GU_PIECE, gu, 4 * rank), (DN_PIECE, dn, GU_CHUNKS + 2 * rank))[part]
        for p in range(shard // size):
            yield (
                source.at[pl.ds(p * size, size), :],
                weight.at[rows_of(owner * shard + p * size, size), :],
                ring.at[place_in_order(at + p)],
            )

    shards = (gu_shard.at[0], dn_shard.at[0])
    others = (gu_other, dn_other)

    def send_shard(part):
        for source, place, sem in shard_chunks(part, shards[part], q):
            pltpu.make_async_remote_copy(
                source, place, shard_send.at[part], sem, device_id=(2 * z + core, z), device_id_type=MESH
            ).start()

    def send_shard_on_call(part):
        pl.semaphore_wait(go.at[part], 1)
        send_shard(part)

    def send_other_on_call(part):
        pltpu.make_async_copy(others[part], others[part], other_recv.at[part]).wait()
        pl.semaphore_wait(go.at[2 + part], 1)
        for source, place, sem in shard_chunks(part, others[part], opposite):
            pltpu.make_async_remote_copy(
                source, place, shard_send.at[2 + part], sem, device_id=(2 * z + core, z), device_id_type=MESH
            ).start()

    def calls(rank):
        gu_call = 4 * (rank - GU_LEAD) - HOP * dist + SLACK
        dn_call = GU_CHUNKS + 2 * rank - DN_LEAD - HOP * dist + SLACK
        return gu_call, dn_call

    rank = rank_of(z, q)
    at_once = rank < AT_ONCE
    is_direct = jnp.logical_not(is_target | goes_by)
    gu_call, dn_call = calls(rank)
    gu_other_call, dn_other_call = calls(rank_of(z, opposite))

    @pl.when(is_target)
    def _():
        for part in range(2):
            for source, place, sem in shard_chunks(part, shards[part], q):
                pltpu.make_async_copy(source, place, sem).start()

    @pl.when(goes_by)
    def _():
        for part in range(2):
            pltpu.make_async_remote_copy(
                shards[part],
                others[part],
                shard_send.at[part],
                other_recv.at[part],
                device_id=(2 * between + core, z),
                device_id_type=MESH,
            ).start()

    @pl.when(is_direct & at_once)
    def _():
        send_shard(0)

    slot_id = lax.broadcasted_iota(jnp.int32, (slots, tok_rows), 0)
    expert_of = slot_id // SLOTS
    slot_of = slot_id - expert_of * SLOTS
    weight_of = jnp.zeros((slots, tok_rows), jnp.float32)
    named = jnp.zeros((slots, tok_rows), jnp.float32)
    for k in range(top):
        hit = routes[k : k + 1, :] == expert_of
        named = jnp.where(hit, 1.0, named)
        weight_of = jnp.where(hit, route_weights[k : k + 1, :], weight_of)
    row_id = lax.broadcasted_iota(jnp.int32, (tok_rows, tok_rows), 0)
    col_id = lax.broadcasted_iota(jnp.int32, (tok_rows, tok_rows), 1)
    above = jnp.where(row_id < col_id, 1.0, 0.0).astype(jnp.bfloat16)
    earlier = dot(named.astype(jnp.bfloat16), above).astype(jnp.int32)
    kept = (named > 0.5) & (earlier == slot_of) & (slot_of < capacity)
    chosen = jnp.where(kept, 1.0, 0.0)
    weight_of = jnp.where(kept, weight_of, 0.0)
    picks = chosen.astype(jnp.bfloat16)
    slot_weight = jnp.sum(weight_of, axis=1, keepdims=True)
    loads[0].wait()
    send_t[...] = dot(picks, tokens[...]).astype(jnp.bfloat16)
    loads[1].wait()
    send_g[...] = (slot_weight * dot(picks, cotangent[...])).astype(jnp.bfloat16)

    @pl.when(is_direct & jnp.logical_not(at_once) & (gu_call < 0))
    def _():
        send_shard_on_call(0)

    @pl.when(is_between & (gu_other_call < 0))
    def _():
        send_other_on_call(0)

    @pl.when(is_direct & (dn_call < 0))
    def _():
        send_shard_on_call(1)

    @pl.when(is_between & (dn_other_call < 0))
    def _():
        send_other_on_call(1)

    gu_call = jnp.where(is_direct & jnp.logical_not(at_once), gu_call, -1)
    dn_call = jnp.where(is_direct, dn_call, -1)
    gu_other_call = jnp.where(is_between, gu_other_call, -1)
    dn_other_call = jnp.where(is_between, dn_other_call, -1)

    mine = rows_of(q * SLOTS, SLOTS)

    def keep_rows(source, place, recv_sem):
        pltpu.make_async_copy(source.at[mine, :], place.at[mine, :], recv_sem).start()

    def send_rows(k, source, place, send_sem, recv_sem):
        other = lax.rem(q + k, n)
        pltpu.make_async_remote_copy(
            source.at[rows_of(other * SLOTS, SLOTS), :],
            place.at[mine, :],
            send_sem,
            recv_sem,
            device_id=(2 * other + core, z),
            device_id_type=MESH,
        ).start()

    def return_rows(source, place, send_sem, recv_sem):
        keep_rows(source, place, recv_sem)
        for dx, dy in FAR_FIRST:
            other = 4 * lax.rem(q // 4 + dy, 4) + lax.rem(lax.rem(q, 4) + dx, 4)
            pltpu.make_async_remote_copy(
                source.at[rows_of(other * SLOTS, SLOTS), :],
                place.at[mine, :],
                send_sem,
                recv_sem,
                device_id=(2 * other + core, z),
                device_id_type=MESH,
            ).start()

    def sent_rows(source, send_sem):
        rest = source.at[pl.ds(0, (n - 1) * SLOTS), :]
        pltpu.make_async_copy(rest, rest, send_sem).wait()

    def arrived_rows(place, recv_sem):
        pltpu.make_async_copy(place, place, recv_sem).wait()

    keep_rows(send_t, in_t, row_recv.at[0])
    keep_rows(send_g, in_g, row_recv.at[1])
    row_call = jnp.minimum(jnp.maximum(ROW_CALL - HOP * dist, 0), own - 2 * ROW_EVERY * (n - 1))

    def gu_chunk(u):
        i = number(u)
        h = jnp.where(i < CHUNKS // 2, 0, 1)
        t = jnp.where(h == 0, i, CHUNKS - 1 - i)
        start = (2 * chip_at(q, t // 4) + h) * shard + lax.rem(t, 4) * GU_PIECE
        return gu.at[rows_of(start, GU_PIECE), :]

    def dn_chunk(u):
        i = number(u)
        h = jnp.where(i < CHUNKS // 2, 0, 1)
        t = jnp.where(h == 0, i, CHUNKS - 1 - i) - GU_CHUNKS
        start = (2 * chip_at(q, t // 2) + h) * shard + lax.rem(t, 2) * DN_PIECE
        return dn.at[rows_of(start, DN_PIECE), :]

    def pass_on(chunk, u):
        i = number(u)

        @pl.when(u < passed)
        def _():
            pltpu.make_async_remote_copy(
                chunk, chunk, ring_send.at[i // 8], ring.at[i], device_id=(me, after), device_id_type=MESH
            ).start()

    def take(chunk, u):
        i = number(u)
        pltpu.make_async_copy(chunk, chunk, ring.at[i]).wait()
        pass_on(chunk, u)
        pltpu.make_async_remote_copy(
            chunk, chunk, sib_send.at[i // 8], sib.at[i // 8], device_id=(sibling, z), device_id_type=MESH
        ).start()

    def call_shards(u):
        def call(r, part):
            chip = chip_at(q, r)
            by = is_opposite(q, chip)
            holder = jnp.where(by, 4 * (q // 4) + lax.rem(chip, 4), chip)

            @pl.when(chip != q)
            def _():
                pl.semaphore_signal(
                    go.at[jnp.where(by, 2 + part, part)],
                    inc=1,
                    device_id=(2 * holder + core, z),
                    device_id_type=MESH,
                )

        j = u // 4 + GU_LEAD
        k = (u - GU_CHUNKS + DN_LEAD) // 2

        @pl.when(is_first & (u == 0))
        def _():
            for r in range(AT_ONCE, GU_LEAD):
                call(r, 0)

        @pl.when(is_first & (lax.rem(u, 4) == 0) & (j < n))
        def _():
            call(j, 0)

        @pl.when(is_first & (lax.rem(u, 2) == 0) & (u >= GU_CHUNKS - DN_LEAD) & (k < n))
        def _():
            call(k, 1)

    def beside(u):
        call_shards(u)

        @pl.when(u == gu_call)
        def _():
            send_shard_on_call(0)

        @pl.when(u == dn_call)
        def _():
            send_shard_on_call(1)

        @pl.when(u == gu_other_call)
        def _():
            send_other_on_call(0)

        @pl.when(u == dn_other_call)
        def _():
            send_other_on_call(1)

        k = (u - row_call) // ROW_EVERY

        @pl.when((u >= row_call) & (lax.rem(u - row_call, ROW_EVERY) == 0))
        def _():
            @pl.when(k < n - 1)
            def _():
                send_rows(k + 1, send_t, in_t, row_send.at[0], row_recv.at[0])

            @pl.when((k >= n - 1) & (k < 2 * (n - 1)))
            def _():
                send_rows(k - n + 2, send_g, in_g, row_send.at[1], row_recv.at[1])

    def wait_group(g, sems):
        group = gu.at[pl.ds(0, 8 * GU_PIECE), :]
        pltpu.make_async_copy(group, group, sems.at[number(8 * g) // 8]).wait()

    def wait_step(g, carry):
        wait_group(g, sib)
        return carry

    tile = min(256, ff)

    def wait_gate_up():
        lax.fori_loop(2 * GU_CHUNKS // 8, CHUNKS // 8, wait_step, 0)
        arrived_rows(in_t, row_recv.at[0])

    def gate_up(j):
        cols = rows_of(j * tile, tile)
        gate[:, cols] = dot(in_t[...], gu[:, cols])
        up[:, cols] = dot(in_t[...], gu[:, rows_of(ff + j * tile, tile)])
        hidden[:, cols] = (jax.nn.silu(gate[:, cols]) * up[:, cols]).astype(jnp.bfloat16)

    other_late = jnp.where(upward, OTHER_UP - OTHER_STEP * dist, OTHER_DOWN - OTHER_STEP * dist)
    gate_up_at = GU_CHUNKS + jnp.maximum(other_late, 0) + MARGIN
    is_early = (gate_up_at + 2 * (ff // tile) < own) & jnp.logical_not(is_first)
    gate_up_at = jnp.where(is_early, gate_up_at, CHUNKS)

    def gu_step(u, carry):
        beside(u)
        take(gu_chunk(u), u)
        return carry

    def dn_step(u, carry):
        beside(u)
        take(dn_chunk(u), u)
        j = (u - gate_up_at) // 2

        @pl.when(u == gate_up_at)
        def _():
            wait_gate_up()

        @pl.when((u >= gate_up_at) & (lax.rem(u - gate_up_at, 2) == 0) & (j < ff // tile))
        def _():
            gate_up(j)

        return carry

    lax.fori_loop(0, GU_CHUNKS, gu_step, 0)
    lax.fori_loop(GU_CHUNKS, own, dn_step, 0)

    def group_step(g, carry):
        wait_group(g, sib)

        def one(k, carry):
            pass_on(dn_chunk(8 * g + k), 8 * g + k)
            return carry

        lax.fori_loop(0, 8, one, 0)
        return carry

    seen = jnp.maximum(own, passed) // 8
    lax.fori_loop(own // 8, seen, group_step, 0)

    @pl.when(jnp.logical_not(is_early))
    def _():
        wait_gate_up()

        def gate_up_step(j, carry):
            gate_up(j)
            return carry

        lax.fori_loop(0, ff // tile, gate_up_step, 0)

    lax.fori_loop(seen, 2 * GU_CHUNKS // 8, wait_step, 0)

    kept_width = width * capacity // SLOTS
    parts = kept_width // WIDE
    row = lax.broadcasted_iota(jnp.int32, (slots, slots), 0)
    col = lax.broadcasted_iota(jnp.int32, (slots, slots), 1)

    def folds(row, col, part):
        r = row // SLOTS * SLOTS + (lax.rem(row, SLOTS) - capacity) * parts + part
        return jnp.where((lax.rem(row, SLOTS) >= capacity) & (col == r), 1.0, 0.0).astype(jnp.bfloat16)

    fold = [folds(row, col, part) for part in range(parts)]

    def packed(value, place):
        last = value(parts).astype(jnp.bfloat16)
        for part in range(parts):
            place[:, part * WIDE : (part + 1) * WIDE] = (value(part) + dot(fold[part], last)).astype(jnp.bfloat16)

    packed(lambda j: dot_nt(hidden[...], dn[j * WIDE : (j + 1) * WIDE, :]), out_s)
    return_rows(out_s, back_o, back_send.at[0], back_recv.at[0])

    arrived_rows(in_g, row_recv.at[1])

    def grad_hidden_step(j, carry):
        cols = rows_of(j * tile, tile)
        grad_hidden = dot(in_g[...], dn[:, cols])
        g = gate[:, cols]
        s = jax.nn.sigmoid(g)
        ggu[:, cols] = (grad_hidden * up[:, cols] * s * (1.0 + g * (1.0 - s))).astype(jnp.bfloat16)
        ggu[:, rows_of(ff + j * tile, tile)] = (grad_hidden * g * s).astype(jnp.bfloat16)
        return carry

    lax.fori_loop(0, ff // tile, grad_hidden_step, 0)
    packed(lambda j: dot_nt(ggu[...], gu[j * WIDE : (j + 1) * WIDE, :]), eg_s)
    return_rows(eg_s, back_g, back_send.at[1], back_recv.at[1])

    by_token = jnp.transpose(weight_of)
    first = by_token.astype(jnp.bfloat16)
    rest = by_token - first.astype(jnp.float32)
    second = rest.astype(jnp.bfloat16)
    third = (rest - second.astype(jnp.float32)).astype(jnp.bfloat16)
    by_slot[...] = jnp.transpose(chosen).astype(jnp.bfloat16)
    arrived_rows(back_o, back_recv.at[0])
    unfold = [folds(col, row, part) for part in range(parts)]
    last = sum(dot(unfold[part], back_o[:, part * WIDE : (part + 1) * WIDE]) for part in range(parts))
    products = jnp.zeros((slots, tok_rows), jnp.float32)
    for part in range(parts + 1):
        cols = slice(part * WIDE, (part + 1) * WIDE)
        out = back_o[:, cols] if part < parts else last.astype(jnp.bfloat16)
        mixed[:, cols] = (dot(first, out) + (dot(second, out) + dot(third, out))).astype(jnp.bfloat16)
        products = products + dot_nt(out, cotangent[:, cols])
    products = jnp.where(kept, products, 0.0)
    for k in range(top):
        hit = routes[k : k + 1, :] == expert_of
        grad_gates[k : k + 1, :] = jnp.sum(jnp.where(hit, products, 0.0), axis=0, keepdims=True)

    def ring_sent(g, carry):
        wait_group(g, ring_send)
        return carry

    def sib_sent(g, carry):
        wait_group(g, sib_send)
        return carry

    lax.fori_loop(0, passed // 8, ring_sent, 0)
    lax.fori_loop(0, own // 8, sib_sent, 0)

    @pl.when(jnp.logical_not(is_target))
    def _():
        for part in range(2):
            pltpu.make_async_copy(others[part], others[part], shard_send.at[part]).wait()

    @pl.when(is_between)
    def _():
        for part in range(2):
            pltpu.make_async_copy(others[part], others[part], shard_send.at[2 + part]).wait()

    sent_rows(send_t, row_send.at[0])
    sent_rows(send_g, row_send.at[1])
    sent_rows(out_s, back_send.at[0])
    sent_rows(eg_s, back_send.at[1])
    arrived_rows(back_g, back_recv.at[1])


def finish(
    capacity,
    mixed_hbm,
    back_hbm,
    by_slot_hbm,
    gates_hbm,
    mixed_out,
    grad_out,
    gates_out,
    mixed,
    back,
    by_slot,
    gates,
    grad,
    sems,
    out_sems,
):
    slots, kept_width = back.shape
    parts = kept_width // WIDE
    get_slot = pltpu.make_async_copy(by_slot_hbm, by_slot, sems.at[parts])
    get_slot.start()
    gets = []
    for part in range(parts):
        cols = slice(part * WIDE, (part + 1) * WIDE)
        gets.append(pltpu.make_async_copy(back_hbm.at[:, cols], back.at[:, cols], sems.at[part]))
        gets[part].start()
    passing = [
        pltpu.make_async_copy(mixed_hbm, mixed, sems.at[parts + 1]),
        pltpu.make_async_copy(gates_hbm, gates, sems.at[parts + 2]),
    ]
    for copy in passing:
        copy.start()
    row = lax.broadcasted_iota(jnp.int32, (slots, slots), 0)
    col = lax.broadcasted_iota(jnp.int32, (slots, slots), 1)
    block = col // SLOTS * SLOTS
    copies = [
        pltpu.make_async_copy(mixed, mixed_out, out_sems.at[parts + 1]),
        pltpu.make_async_copy(gates, gates_out, out_sems.at[parts + 2]),
    ]
    get_slot.wait()
    last = jnp.zeros((slots, WIDE), jnp.float32)
    for part in range(parts + 1):
        cols = slice(part * WIDE, (part + 1) * WIDE)
        if part < parts:
            gets[part].wait()
            rows = back[:, cols]
            source = block + (lax.rem(col, SLOTS) - capacity) * parts + part
            unfold = jnp.where((lax.rem(col, SLOTS) >= capacity) & (row == source), 1.0, 0.0)
            last = last + dot(unfold.astype(jnp.bfloat16), rows)
        else:
            rows = last.astype(jnp.bfloat16)
        grad[:, cols] = dot(by_slot[...], rows).astype(jnp.bfloat16)
        copy = pltpu.make_async_copy(grad.at[:, cols], grad_out.at[:, cols], out_sems.at[part])
        copy.start()
        copies.append(copy)
        if part < 2:
            passing[part].wait()
            copies[part].start()
    for copy in copies:
        copy.wait()


def on_device(tokens, cotangent, routes, route_weights, gate_up_weight, down_weight):
    n = lax.axis_size("expert")
    tok_rows, width = tokens.shape
    top = routes.shape[1]
    shard, ff = down_weight.shape[1:]
    capacity = 3 * tok_rows // 32
    slots = n * SLOTS
    rows = pltpu.VMEM((slots, width), jnp.bfloat16)
    dma = pltpu.SemaphoreType.DMA
    hbm = pl.BlockSpec(memory_space=pl.ANY)
    vmem = pl.BlockSpec(memory_space=pltpu.VMEM)
    kept_width = width * capacity // SLOTS
    packed_rows = pltpu.VMEM((slots, kept_width), jnp.bfloat16)
    mixed, back, by_slot, grad_gates = pl.pallas_call(
        functools.partial(kernel, n, capacity),
        out_shape=(
            jax.ShapeDtypeStruct((tok_rows, width), jnp.bfloat16),
            jax.ShapeDtypeStruct((slots, kept_width), jnp.bfloat16),
            jax.ShapeDtypeStruct((tok_rows, slots), jnp.bfloat16),
            jax.ShapeDtypeStruct((top, tok_rows), jnp.float32),
        ),
        in_specs=[hbm, hbm, vmem, vmem, hbm, hbm],
        out_specs=[vmem] * 4,
        scratch_shapes=[
            pltpu.VMEM((tok_rows, width), jnp.bfloat16),
            pltpu.VMEM((tok_rows, width), jnp.bfloat16),
            pltpu.VMEM((width, 2 * ff), jnp.bfloat16),
            pltpu.VMEM((width, ff), jnp.bfloat16),
            rows,
            rows,
            rows,
            rows,
            pltpu.VMEM((slots, ff), jnp.float32),
            pltpu.VMEM((slots, ff), jnp.float32),
            pltpu.VMEM((slots, ff), jnp.bfloat16),
            pltpu.VMEM((slots, 2 * ff), jnp.bfloat16),
            packed_rows,
            packed_rows,
            packed_rows,
            pltpu.VMEM((shard, 2 * ff), jnp.bfloat16),
            pltpu.VMEM((shard, ff), jnp.bfloat16),
            dma((2,)),
            dma((CHUNKS,)),
            dma((CHUNKS // 8,)),
            dma((CHUNKS // 8,)),
            dma((CHUNKS // 8,)),
            dma((4,)),
            dma((2,)),
            dma((2,)),
            dma((2,)),
            dma((2,)),
            dma((2,)),
            pltpu.SemaphoreType.REGULAR((4,)),
        ],
        compiler_params=pltpu.CompilerParams(
            collective_id=0, has_side_effects=True, vmem_limit_bytes=56 * 1024 * 1024
        ),
    )(tokens, cotangent, routes.T, route_weights.T, gate_up_weight, down_weight)
    mixed, grad_tokens, grad_gates = pl.pallas_call(
        functools.partial(finish, capacity),
        out_shape=(
            jax.ShapeDtypeStruct((tok_rows, width), jnp.bfloat16),
            jax.ShapeDtypeStruct((tok_rows, width), jnp.bfloat16),
            jax.ShapeDtypeStruct((top, tok_rows), jnp.float32),
        ),
        in_specs=[hbm] * 4,
        out_specs=[hbm] * 3,
        scratch_shapes=[
            pltpu.VMEM((tok_rows, width), jnp.bfloat16),
            pltpu.VMEM((slots, kept_width), jnp.bfloat16),
            pltpu.VMEM((tok_rows, slots), jnp.bfloat16),
            pltpu.VMEM((top, tok_rows), jnp.float32),
            pltpu.VMEM((tok_rows, width), jnp.bfloat16),
            dma((3 + kept_width // WIDE,)),
            dma((3 + kept_width // WIDE,)),
        ],
        compiler_params=pltpu.CompilerParams(vmem_limit_bytes=56 * 1024 * 1024),
    )(mixed, back, by_slot, grad_gates)
    return mixed, grad_tokens, grad_gates.T


def solution(mesh):
    rows = P(("fsdp", "expert"), None)
    weight = P("expert", "fsdp", None)
    return jax.shard_map(
        on_device,
        mesh=mesh,
        in_specs=(rows, rows, rows, rows, weight, weight),
        out_specs=(rows, rows, rows),
        check_vma=False,
    )
```

```python
import functools

import jax
import jax.numpy as jnp
from jax import lax
from jax.experimental import pallas as pl
from jax.experimental.pallas import tpu as pltpu
from jax.sharding import PartitionSpec as P

MESH = pl.DeviceIdType.MESH
SLOTS = 16
GU_PIECE = 16
DN_PIECE = 32
GU_CHUNKS = 64
CHUNKS = 3 * GU_CHUNKS
MEET_FIRST, MEET_STEP = 130, 5
AT_ONCE, GU_LEAD, DN_LEAD = 7, 8, 16
HOP, SLACK = 6, 8
ROW_CALL, ROW_EVERY = 110, 2
OTHER_UP, OTHER_DOWN, OTHER_STEP = 77, 98, 11
MARGIN = 10
PREPARE_AT = 32
WIDE = 512
FAR_FIRST = sorted(
    ((k % 4, k // 4) for k in range(1, 16)),
    key=lambda step: -sum(min(a, 4 - a) for a in step),
)
NT = (((1,), (1,)), ((), ()))


def dot(a, b):
    return jnp.dot(a, b, preferred_element_type=jnp.float32)


def dot_nt(a, b):
    return lax.dot_general(a, b, NT, preferred_element_type=jnp.float32)


def rows_of(start, size):
    return pl.ds(pl.multiple_of(start, size), size)


def nearest_row(q, h):
    y = q // 4
    a = lax.rem(2 * h - y + 4, 4)
    b = lax.rem(2 * h + 1 - y + 4, 4)
    return jnp.where(jnp.minimum(a, 4 - a) <= jnp.minimum(b, 4 - b), 2 * h, 2 * h + 1)


def chip_at(q, r):
    m = r // 3
    turn = r - 3 * m
    beyond = (turn == 2) | ((turn == 0) & (m >= 3))
    k_beyond = jnp.where(turn == 2, m, m + 2)
    k_near = jnp.where(turn == 1, jnp.where(m == 0, 1, m + 3), m + jnp.where(m > 0, 1, 0))
    k = jnp.where(beyond, k_beyond, k_near)
    h = jnp.where(beyond, 1 - q // 8, q // 8)
    near = nearest_row(q, h)
    row = jnp.where(k < 4, near, 4 * h + 1 - near)
    d = lax.rem(k, 4)
    x = lax.rem(lax.rem(q, 4) + d + jnp.where(d == 2, 1, 0) - jnp.where(d == 3, 1, 0), 4)
    return 4 * row + x


def rank_of(q, c):
    near = nearest_row(q, c // 8)
    off = lax.rem(lax.rem(c, 4) - lax.rem(q, 4) + 4, 4)
    d = off - jnp.where(off == 3, 1, 0) + jnp.where(off == 2, 1, 0)
    k = jnp.where(c // 4 == near, 0, 4) + d
    of_near = jnp.where(k < 2, k, jnp.where(k < 4, 3 * k - 3, 3 * k - 8))
    of_beyond = jnp.where(k < 5, 3 * k + 2, 3 * k - 6)
    return jnp.where(c // 8 == q // 8, of_near, of_beyond)


def is_opposite(q, c):
    return (lax.rem(c // 4 - q // 4 + 4, 4) == 2) & (lax.rem(c, 4) != lax.rem(q, 4))


def kernel(
    n,
    capacity,
    tokens_hbm,
    cotangent_hbm,
    routes,
    route_weights,
    gu_shard,
    dn_shard,
    mixed,
    back_g,
    by_slot,
    grad_gates,
    tokens,
    cotangent,
    gu,
    dn,
    send_t,
    send_g,
    in_t,
    in_g,
    gate,
    up,
    hidden,
    ggu,
    out_s,
    eg_s,
    back_o,
    gu_other,
    dn_other,
    weight_of,
    chosen,
    load,
    ring,
    sib,
    ring_send,
    sib_send,
    shard_send,
    row_recv,
    row_send,
    back_recv,
    back_send,
    other_recv,
    go,
):
    tok_rows, width = tokens.shape
    top = routes.shape[0]
    shard = gu_shard.shape[1]
    ff = dn_shard.shape[2]
    slots = n * SLOTS
    me = lax.axis_index("fsdp")
    z = lax.axis_index("expert")
    q = me // 2
    core = lax.rem(me, 2)
    sibling = me + 1 - 2 * core
    upward = core == 0
    after = lax.rem(z + 1 + core * (n - 2), n)
    before = lax.rem(z + n - 1 - core * (n - 2), n)

    loads = (
        pltpu.make_async_copy(tokens_hbm, tokens, load.at[0]),
        pltpu.make_async_copy(cotangent_hbm, cotangent, load.at[1]),
    )
    for copy in loads:
        copy.start()

    barrier = pltpu.get_barrier_semaphore()

    def greet(k, carry):
        other = 2 * lax.rem(q + k, n) + core
        pl.semaphore_signal(barrier, inc=1, device_id=(other, z), device_id_type=MESH)
        return carry

    pl.semaphore_signal(barrier, inc=1, device_id=(me, after), device_id_type=MESH)
    pl.semaphore_signal(barrier, inc=1, device_id=(me, before), device_id_type=MESH)
    pl.semaphore_signal(barrier, inc=1, device_id=(sibling, z), device_id_type=MESH)
    lax.fori_loop(1, n, greet, 0)

    pl.semaphore_wait(barrier, n + 2)

    def meet(d):
        return jnp.minimum(jnp.maximum(8 * ((MEET_FIRST - MEET_STEP * d + 4) // 8), GU_CHUNKS), 2 * GU_CHUNKS)

    d = lax.rem(z - q + n, n)
    dist = jnp.where(upward, d, lax.rem(n - d, n))
    next_d = jnp.where(upward, d + 1, lax.rem(d + n - 1, n))
    is_first = d == 0
    own = jnp.where(is_first, CHUNKS // 2, jnp.where(upward, meet(d), CHUNKS - meet(d)))
    passed = jnp.where(upward, meet(next_d), CHUNKS - meet(next_d))
    passed = jnp.where((next_d == 0) | (next_d == n), 0, passed)

    def number(u):
        return jnp.where(upward, u, CHUNKS - 1 - u)

    is_target = q == z
    opposite = lax.rem(q + n // 2, n)
    goes_by = is_opposite(z, q)
    is_between = is_opposite(z, opposite)
    between = 4 * (z // 4) + lax.rem(q, 4)

    def place_in_order(t):
        return jnp.where(upward, t, CHUNKS - 1 - t)

    def shard_chunks(part, source, chip):
        owner, rank = 2 * chip + core, rank_of(z, chip)
        size, weight, at = ((GU_PIECE, gu, 4 * rank), (DN_PIECE, dn, GU_CHUNKS + 2 * rank))[part]
        for p in range(shard // size):
            yield (
                source.at[pl.ds(p * size, size), :],
                weight.at[rows_of(owner * shard + p * size, size), :],
                ring.at[place_in_order(at + p)],
            )

    shards = (gu_shard.at[0], dn_shard.at[0])
    others = (gu_other, dn_other)

    def send_shard(part):
        for source, place, sem in shard_chunks(part, shards[part], q):
            pltpu.make_async_remote_copy(
                source, place, shard_send.at[part], sem, device_id=(2 * z + core, z), device_id_type=MESH
            ).start()

    def send_shard_on_call(part):
        pl.semaphore_wait(go.at[part], 1)
        send_shard(part)

    def send_other_on_call(part):
        pltpu.make_async_copy(others[part], others[part], other_recv.at[part]).wait()
        pl.semaphore_wait(go.at[2 + part], 1)
        for source, place, sem in shard_chunks(part, others[part], opposite):
            pltpu.make_async_remote_copy(
                source, place, shard_send.at[2 + part], sem, device_id=(2 * z + core, z), device_id_type=MESH
            ).start()

    def calls(rank):
        gu_call = 4 * (rank - GU_LEAD) - HOP * dist + SLACK
        dn_call = GU_CHUNKS + 2 * rank - DN_LEAD - HOP * dist + SLACK
        return gu_call, dn_call

    rank = rank_of(z, q)
    at_once = rank < AT_ONCE
    is_direct = jnp.logical_not(is_target | goes_by)
    gu_call, dn_call = calls(rank)
    gu_other_call, dn_other_call = calls(rank_of(z, opposite))

    @pl.when(is_target)
    def _():
        for part in range(2):
            for source, place, sem in shard_chunks(part, shards[part], q):
                pltpu.make_async_copy(source, place, sem).start()

    @pl.when(goes_by)
    def _():
        for part in range(2):
            pltpu.make_async_remote_copy(
                shards[part],
                others[part],
                shard_send.at[part],
                other_recv.at[part],
                device_id=(2 * between + core, z),
                device_id_type=MESH,
            ).start()

    @pl.when(is_direct & at_once)
    def _():
        send_shard(0)

    expert_of = lax.broadcasted_iota(jnp.int32, (slots, tok_rows), 0) // SLOTS

    def prepare_rows():
        slot_of = lax.broadcasted_iota(jnp.int32, (slots, tok_rows), 0) - expert_of * SLOTS
        weight = jnp.zeros((slots, tok_rows), jnp.float32)
        named = jnp.zeros((slots, tok_rows), jnp.float32)
        for k in range(top):
            hit = routes[k : k + 1, :] == expert_of
            named = jnp.where(hit, 1.0, named)
            weight = jnp.where(hit, route_weights[k : k + 1, :], weight)
        row_id = lax.broadcasted_iota(jnp.int32, (tok_rows, tok_rows), 0)
        col_id = lax.broadcasted_iota(jnp.int32, (tok_rows, tok_rows), 1)
        above = jnp.where(row_id < col_id, 1.0, 0.0).astype(jnp.bfloat16)
        earlier = dot(named.astype(jnp.bfloat16), above).astype(jnp.int32)
        kept = (named > 0.5) & (earlier == slot_of) & (slot_of < capacity)
        weight = jnp.where(kept, weight, 0.0)
        weight_of[...] = weight
        chosen[...] = jnp.where(kept, 1.0, 0.0)
        picks = chosen[...].astype(jnp.bfloat16)
        slot_weight = jnp.sum(weight, axis=1, keepdims=True)
        loads[0].wait()
        send_t[...] = dot(picks, tokens[...]).astype(jnp.bfloat16)
        loads[1].wait()
        send_g[...] = (slot_weight * dot(picks, cotangent[...])).astype(jnp.bfloat16)

    @pl.when(jnp.logical_not(is_first))
    def _():
        prepare_rows()

    @pl.when(is_direct & jnp.logical_not(at_once) & (gu_call < 0))
    def _():
        send_shard_on_call(0)

    @pl.when(is_between & (gu_other_call < 0))
    def _():
        send_other_on_call(0)

    @pl.when(is_direct & (dn_call < 0))
    def _():
        send_shard_on_call(1)

    @pl.when(is_between & (dn_other_call < 0))
    def _():
        send_other_on_call(1)

    gu_call = jnp.where(is_direct & jnp.logical_not(at_once), gu_call, -1)
    dn_call = jnp.where(is_direct, dn_call, -1)
    gu_other_call = jnp.where(is_between, gu_other_call, -1)
    dn_other_call = jnp.where(is_between, dn_other_call, -1)

    mine = rows_of(q * SLOTS, SLOTS)

    def keep_rows(source, place, recv_sem):
        pltpu.make_async_copy(source.at[mine, :], place.at[mine, :], recv_sem).start()

    def send_rows(k, source, place, send_sem, recv_sem):
        other = lax.rem(q + k, n)
        pltpu.make_async_remote_copy(
            source.at[rows_of(other * SLOTS, SLOTS), :],
            place.at[mine, :],
            send_sem,
            recv_sem,
            device_id=(2 * other + core, z),
            device_id_type=MESH,
        ).start()

    def return_rows(source, place, send_sem, recv_sem):
        keep_rows(source, place, recv_sem)
        for dx, dy in FAR_FIRST:
            other = 4 * lax.rem(q // 4 + dy, 4) + lax.rem(lax.rem(q, 4) + dx, 4)
            pltpu.make_async_remote_copy(
                source.at[rows_of(other * SLOTS, SLOTS), :],
                place.at[mine, :],
                send_sem,
                recv_sem,
                device_id=(2 * other + core, z),
                device_id_type=MESH,
            ).start()

    def sent_rows(source, send_sem):
        rest = source.at[pl.ds(0, (n - 1) * SLOTS), :]
        pltpu.make_async_copy(rest, rest, send_sem).wait()

    def arrived_rows(place, recv_sem):
        pltpu.make_async_copy(place, place, recv_sem).wait()

    row_call = jnp.minimum(jnp.maximum(ROW_CALL - HOP * dist, 0), own - 2 * ROW_EVERY * (n - 1))

    def gu_chunk(u):
        i = number(u)
        h = jnp.where(i < CHUNKS // 2, 0, 1)
        t = jnp.where(h == 0, i, CHUNKS - 1 - i)
        start = (2 * chip_at(q, t // 4) + h) * shard + lax.rem(t, 4) * GU_PIECE
        return gu.at[rows_of(start, GU_PIECE), :]

    def dn_chunk(u):
        i = number(u)
        h = jnp.where(i < CHUNKS // 2, 0, 1)
        t = jnp.where(h == 0, i, CHUNKS - 1 - i) - GU_CHUNKS
        start = (2 * chip_at(q, t // 2) + h) * shard + lax.rem(t, 2) * DN_PIECE
        return dn.at[rows_of(start, DN_PIECE), :]

    def pass_on(chunk, u):
        i = number(u)

        @pl.when(u < passed)
        def _():
            pltpu.make_async_remote_copy(
                chunk, chunk, ring_send.at[i // 8], ring.at[i], device_id=(me, after), device_id_type=MESH
            ).start()

    def take(chunk, u):
        i = number(u)
        pltpu.make_async_copy(chunk, chunk, ring.at[i]).wait()
        pass_on(chunk, u)
        pltpu.make_async_remote_copy(
            chunk, chunk, sib_send.at[i // 8], sib.at[i // 8], device_id=(sibling, z), device_id_type=MESH
        ).start()

    def call_shards(u):
        def call(r, part):
            chip = chip_at(q, r)
            by = is_opposite(q, chip)
            holder = jnp.where(by, 4 * (q // 4) + lax.rem(chip, 4), chip)

            @pl.when(chip != q)
            def _():
                pl.semaphore_signal(
                    go.at[jnp.where(by, 2 + part, part)],
                    inc=1,
                    device_id=(2 * holder + core, z),
                    device_id_type=MESH,
                )

        j = u // 4 + GU_LEAD
        k = (u - GU_CHUNKS + DN_LEAD) // 2

        @pl.when(is_first & (u == 0))
        def _():
            for r in range(AT_ONCE, GU_LEAD):
                call(r, 0)

        @pl.when(is_first & (lax.rem(u, 4) == 0) & (j < n))
        def _():
            call(j, 0)

        @pl.when(is_first & (lax.rem(u, 2) == 0) & (u >= GU_CHUNKS - DN_LEAD) & (k < n))
        def _():
            call(k, 1)

    def beside(u):
        call_shards(u)

        @pl.when(is_first & (u == PREPARE_AT))
        def _():
            prepare_rows()

        @pl.when(u == gu_call)
        def _():
            send_shard_on_call(0)

        @pl.when(u == dn_call)
        def _():
            send_shard_on_call(1)

        @pl.when(u == gu_other_call)
        def _():
            send_other_on_call(0)

        @pl.when(u == dn_other_call)
        def _():
            send_other_on_call(1)

        k = (u - row_call) // ROW_EVERY

        @pl.when((u >= row_call) & (lax.rem(u - row_call, ROW_EVERY) == 0))
        def _():
            @pl.when(k == 0)
            def _():
                keep_rows(send_t, in_t, row_recv.at[0])
                keep_rows(send_g, in_g, row_recv.at[1])

            @pl.when(k < n - 1)
            def _():
                send_rows(k + 1, send_t, in_t, row_send.at[0], row_recv.at[0])

            @pl.when((k >= n - 1) & (k < 2 * (n - 1)))
            def _():
                send_rows(k - n + 2, send_g, in_g, row_send.at[1], row_recv.at[1])

    def wait_group(g, sems):
        group = gu.at[pl.ds(0, 8 * GU_PIECE), :]
        pltpu.make_async_copy(group, group, sems.at[number(8 * g) // 8]).wait()

    def wait_step(g, carry):
        wait_group(g, sib)
        return carry

    tile = min(256, ff)

    def wait_gate_up():
        lax.fori_loop(2 * GU_CHUNKS // 8, CHUNKS // 8, wait_step, 0)
        arrived_rows(in_t, row_recv.at[0])

    def gate_up(j):
        cols = rows_of(j * tile, tile)
        gate[:, cols] = dot(in_t[...], gu[:, cols])
        up[:, cols] = dot(in_t[...], gu[:, rows_of(ff + j * tile, tile)])
        hidden[:, cols] = (jax.nn.silu(gate[:, cols]) * up[:, cols]).astype(jnp.bfloat16)

    other_late = jnp.where(upward, OTHER_UP - OTHER_STEP * dist, OTHER_DOWN - OTHER_STEP * dist)
    gate_up_at = GU_CHUNKS + jnp.maximum(other_late, 0) + MARGIN
    is_early = (gate_up_at + 2 * (ff // tile) < own) & jnp.logical_not(is_first)
    gate_up_at = jnp.where(is_early, gate_up_at, CHUNKS)

    def gu_step(u, carry):
        beside(u)
        take(gu_chunk(u), u)
        return carry

    def dn_step(u, carry):
        beside(u)
        take(dn_chunk(u), u)
        j = (u - gate_up_at) // 2

        @pl.when(u == gate_up_at)
        def _():
            wait_gate_up()

        @pl.when((u >= gate_up_at) & (lax.rem(u - gate_up_at, 2) == 0) & (j < ff // tile))
        def _():
            gate_up(j)

        return carry

    lax.fori_loop(0, GU_CHUNKS, gu_step, 0)
    lax.fori_loop(GU_CHUNKS, own, dn_step, 0)

    def group_step(g, carry):
        wait_group(g, sib)

        def one(k, carry):
            pass_on(dn_chunk(8 * g + k), 8 * g + k)
            return carry

        lax.fori_loop(0, 8, one, 0)
        return carry

    seen = jnp.maximum(own, passed) // 8
    lax.fori_loop(own // 8, seen, group_step, 0)

    @pl.when(jnp.logical_not(is_early))
    def _():
        wait_gate_up()

        def gate_up_step(j, carry):
            gate_up(j)
            return carry

        lax.fori_loop(0, ff // tile, gate_up_step, 0)

    lax.fori_loop(seen, 2 * GU_CHUNKS // 8, wait_step, 0)

    kept_width = width * capacity // SLOTS
    parts = kept_width // WIDE
    row = lax.broadcasted_iota(jnp.int32, (slots, slots), 0)
    col = lax.broadcasted_iota(jnp.int32, (slots, slots), 1)

    def folds(row, col, part):
        r = row // SLOTS * SLOTS + (lax.rem(row, SLOTS) - capacity) * parts + part
        return jnp.where((lax.rem(row, SLOTS) >= capacity) & (col == r), 1.0, 0.0).astype(jnp.bfloat16)

    fold = [folds(row, col, part) for part in range(parts)]

    def packed(value, place):
        last = value(parts).astype(jnp.bfloat16)
        for part in range(parts):
            place[:, part * WIDE : (part + 1) * WIDE] = (value(part) + dot(fold[part], last)).astype(jnp.bfloat16)

    packed(lambda j: dot_nt(hidden[...], dn[j * WIDE : (j + 1) * WIDE, :]), out_s)
    return_rows(out_s, back_o, back_send.at[0], back_recv.at[0])

    arrived_rows(in_g, row_recv.at[1])

    def grad_hidden_step(j, carry):
        cols = rows_of(j * tile, tile)
        grad_hidden = dot(in_g[...], dn[:, cols])
        g = gate[:, cols]
        s = jax.nn.sigmoid(g)
        ggu[:, cols] = (grad_hidden * up[:, cols] * s * (1.0 + g * (1.0 - s))).astype(jnp.bfloat16)
        ggu[:, rows_of(ff + j * tile, tile)] = (grad_hidden * g * s).astype(jnp.bfloat16)
        return carry

    lax.fori_loop(0, ff // tile, grad_hidden_step, 0)
    packed(lambda j: dot_nt(ggu[...], gu[j * WIDE : (j + 1) * WIDE, :]), eg_s)
    return_rows(eg_s, back_g, back_send.at[1], back_recv.at[1])

    by_token = jnp.transpose(weight_of[...])
    first = by_token.astype(jnp.bfloat16)
    rest = by_token - first.astype(jnp.float32)
    second = rest.astype(jnp.bfloat16)
    third = (rest - second.astype(jnp.float32)).astype(jnp.bfloat16)
    by_slot[...] = jnp.transpose(chosen[...]).astype(jnp.bfloat16)
    arrived_rows(back_o, back_recv.at[0])
    unfold = [folds(col, row, part) for part in range(parts)]
    last = sum(dot(unfold[part], back_o[:, part * WIDE : (part + 1) * WIDE]) for part in range(parts))
    products = jnp.zeros((slots, tok_rows), jnp.float32)
    for part in range(parts + 1):
        cols = slice(part * WIDE, (part + 1) * WIDE)
        out = back_o[:, cols] if part < parts else last.astype(jnp.bfloat16)
        mixed[:, cols] = (dot(first, out) + (dot(second, out) + dot(third, out))).astype(jnp.bfloat16)
        products = products + dot_nt(out, cotangent[:, cols])
    products = products * chosen[...]
    for k in range(top):
        hit = routes[k : k + 1, :] == expert_of
        grad_gates[k : k + 1, :] = jnp.sum(jnp.where(hit, products, 0.0), axis=0, keepdims=True)

    def ring_sent(g, carry):
        wait_group(g, ring_send)
        return carry

    def sib_sent(g, carry):
        wait_group(g, sib_send)
        return carry

    lax.fori_loop(0, passed // 8, ring_sent, 0)
    lax.fori_loop(0, own // 8, sib_sent, 0)

    @pl.when(jnp.logical_not(is_target))
    def _():
        for part in range(2):
            pltpu.make_async_copy(others[part], others[part], shard_send.at[part]).wait()

    @pl.when(is_between)
    def _():
        for part in range(2):
            pltpu.make_async_copy(others[part], others[part], shard_send.at[2 + part]).wait()

    sent_rows(send_t, row_send.at[0])
    sent_rows(send_g, row_send.at[1])
    sent_rows(out_s, back_send.at[0])
    sent_rows(eg_s, back_send.at[1])
    arrived_rows(back_g, back_recv.at[1])


def finish(
    capacity,
    mixed_hbm,
    back_hbm,
    by_slot_hbm,
    gates_hbm,
    mixed_out,
    grad_out,
    gates_out,
    mixed,
    back,
    by_slot,
    gates,
    grad,
    sems,
    out_sems,
):
    slots, kept_width = back.shape
    parts = kept_width // WIDE
    get_slot = pltpu.make_async_copy(by_slot_hbm, by_slot, sems.at[parts])
    get_slot.start()
    gets = []
    for part in range(parts):
        cols = slice(part * WIDE, (part + 1) * WIDE)
        gets.append(pltpu.make_async_copy(back_hbm.at[:, cols], back.at[:, cols], sems.at[part]))
        gets[part].start()
    passing = [
        pltpu.make_async_copy(mixed_hbm, mixed, sems.at[parts + 1]),
        pltpu.make_async_copy(gates_hbm, gates, sems.at[parts + 2]),
    ]
    for copy in passing:
        copy.start()
    row = lax.broadcasted_iota(jnp.int32, (slots, slots), 0)
    col = lax.broadcasted_iota(jnp.int32, (slots, slots), 1)
    block = col // SLOTS * SLOTS
    copies = [
        pltpu.make_async_copy(mixed, mixed_out, out_sems.at[parts + 1]),
        pltpu.make_async_copy(gates, gates_out, out_sems.at[parts + 2]),
    ]
    get_slot.wait()
    last = jnp.zeros((slots, WIDE), jnp.float32)
    for part in range(parts + 1):
        cols = slice(part * WIDE, (part + 1) * WIDE)
        if part < parts:
            gets[part].wait()
            rows = back[:, cols]
            source = block + (lax.rem(col, SLOTS) - capacity) * parts + part
            unfold = jnp.where((lax.rem(col, SLOTS) >= capacity) & (row == source), 1.0, 0.0)
            last = last + dot(unfold.astype(jnp.bfloat16), rows)
        else:
            rows = last.astype(jnp.bfloat16)
        grad[:, cols] = dot(by_slot[...], rows).astype(jnp.bfloat16)
        copy = pltpu.make_async_copy(grad.at[:, cols], grad_out.at[:, cols], out_sems.at[part])
        copy.start()
        copies.append(copy)
        if part < 2:
            passing[part].wait()
            copies[part].start()
    for copy in copies:
        copy.wait()


def on_device(tokens, cotangent, routes, route_weights, gate_up_weight, down_weight):
    n = lax.axis_size("expert")
    tok_rows, width = tokens.shape
    top = routes.shape[1]
    shard, ff = down_weight.shape[1:]
    capacity = 3 * tok_rows // 32
    slots = n * SLOTS
    rows = pltpu.VMEM((slots, width), jnp.bfloat16)
    dma = pltpu.SemaphoreType.DMA
    hbm = pl.BlockSpec(memory_space=pl.ANY)
    vmem = pl.BlockSpec(memory_space=pltpu.VMEM)
    kept_width = width * capacity // SLOTS
    packed_rows = pltpu.VMEM((slots, kept_width), jnp.bfloat16)
    mixed, back, by_slot, grad_gates = pl.pallas_call(
        functools.partial(kernel, n, capacity),
        out_shape=(
            jax.ShapeDtypeStruct((tok_rows, width), jnp.bfloat16),
            jax.ShapeDtypeStruct((slots, kept_width), jnp.bfloat16),
            jax.ShapeDtypeStruct((tok_rows, slots), jnp.bfloat16),
            jax.ShapeDtypeStruct((top, tok_rows), jnp.float32),
        ),
        in_specs=[hbm, hbm, vmem, vmem, hbm, hbm],
        out_specs=[vmem] * 4,
        scratch_shapes=[
            pltpu.VMEM((tok_rows, width), jnp.bfloat16),
            pltpu.VMEM((tok_rows, width), jnp.bfloat16),
            pltpu.VMEM((width, 2 * ff), jnp.bfloat16),
            pltpu.VMEM((width, ff), jnp.bfloat16),
            rows,
            rows,
            rows,
            rows,
            pltpu.VMEM((slots, ff), jnp.float32),
            pltpu.VMEM((slots, ff), jnp.float32),
            pltpu.VMEM((slots, ff), jnp.bfloat16),
            pltpu.VMEM((slots, 2 * ff), jnp.bfloat16),
            packed_rows,
            packed_rows,
            packed_rows,
            pltpu.VMEM((shard, 2 * ff), jnp.bfloat16),
            pltpu.VMEM((shard, ff), jnp.bfloat16),
            pltpu.VMEM((slots, tok_rows), jnp.float32),
            pltpu.VMEM((slots, tok_rows), jnp.float32),
            dma((2,)),
            dma((CHUNKS,)),
            dma((CHUNKS // 8,)),
            dma((CHUNKS // 8,)),
            dma((CHUNKS // 8,)),
            dma((4,)),
            dma((2,)),
            dma((2,)),
            dma((2,)),
            dma((2,)),
            dma((2,)),
            pltpu.SemaphoreType.REGULAR((4,)),
        ],
        compiler_params=pltpu.CompilerParams(
            collective_id=0, has_side_effects=True, vmem_limit_bytes=56 * 1024 * 1024
        ),
    )(tokens, cotangent, routes.T, route_weights.T, gate_up_weight, down_weight)
    mixed, grad_tokens, grad_gates = pl.pallas_call(
        functools.partial(finish, capacity),
        out_shape=(
            jax.ShapeDtypeStruct((tok_rows, width), jnp.bfloat16),
            jax.ShapeDtypeStruct((tok_rows, width), jnp.bfloat16),
            jax.ShapeDtypeStruct((top, tok_rows), jnp.float32),
        ),
        in_specs=[hbm] * 4,
        out_specs=[hbm] * 3,
        scratch_shapes=[
            pltpu.VMEM((tok_rows, width), jnp.bfloat16),
            pltpu.VMEM((slots, kept_width), jnp.bfloat16),
            pltpu.VMEM((tok_rows, slots), jnp.bfloat16),
            pltpu.VMEM((top, tok_rows), jnp.float32),
            pltpu.VMEM((tok_rows, width), jnp.bfloat16),
            dma((3 + kept_width // WIDE,)),
            dma((3 + kept_width // WIDE,)),
        ],
        compiler_params=pltpu.CompilerParams(vmem_limit_bytes=56 * 1024 * 1024),
    )(mixed, back, by_slot, grad_gates)
    return mixed, grad_tokens, grad_gates.T


def solution(mesh):
    rows = P(("fsdp", "expert"), None)
    weight = P("expert", "fsdp", None)
    return jax.shard_map(
        on_device,
        mesh=mesh,
        in_specs=(rows, rows, rows, rows, weight, weight),
        out_specs=(rows, rows, rows),
        check_vma=False,
    )
```
